512 devices in a mesh: tile: 64 (over x, y, core), mem: 8 (over z).
Axes of the slice: x: 4, y: 8, z: 8, core: 2. Of those that a mesh axis runs over, the one named last changes fastest.
Arguments:
- perturb: bfloat16 [48, 2, 16, 8192], P('mem', None, None, 'tile'), may hold values from -6 to 6
- control: float32 [48, 2, 16, 8192], P('mem', None, None, 'tile'), may hold values from -6 to 6
- obs_cell: int32 [64, 64, 16], P('tile'), may hold values from 0 to 3966, as said below
- obs_count: int32 [64, 64], P('tile'), may hold values from 0 to 16, as said below
- obs_frac: float32 [64, 2, 64, 16], P('tile'), may hold values from 0 to 1
- obs_innov: float32 [64, 64, 16], P('tile'), may hold values from -6 to 6
- obs_prec: float32 [64, 64, 16], P('tile'), may hold values from 1 to 10
Outputs:
- gradient: float32 [48, 2, 16, 8192], P('mem', None, None, 'tile')
The draws below stay inside these ranges and needn't reach their ends.
Inputs may be any that keep to these rules, and one draw needn't show every extreme that they name: `obs_count`: in every draw some owner tile receives 16 live slots from every holder tile. `obs_cell`: each corner has row below 15 and column below 127, so its stencil lies in the owner tile.
All inputs are finite; a program needn't handle non-finite values.
Results may differ from the reference program's by a relative error of at most 0.0003.
Values may be sent and summed in bfloat16 or wider, within the bound.
No kernel may reach another device: no remote copies, remote signals or barrier semaphores. Data moves between devices by JAX's collectives and lax.ppermute only.
A program may use at most 64 MiB of HBM per device.

```python
import math
import jax
import jax.numpy as jnp
from jax import lax

LEV = 2
MEMBERS = 48
CX = 128
NY = 16
YSCALE = 1
NX = 8192
CAP = 16
N_TILE = 64


def draw_obs_count(key, part):
    key = jax.random.fold_in(key, 11)
    key_base, key_level, key_full = jax.random.split(key, 3)
    base_count = jax.random.randint(key_base, (N_TILE, N_TILE), 0, CAP + 1)
    level_mult = jax.random.randint(key_level, (N_TILE,), 2, 6)
    counts = jnp.minimum(CAP, base_count * level_mult[None, :] // 3)
    full_owner = jax.random.randint(key_full, (), 0, N_TILE)
    counts = jnp.where(jnp.arange(N_TILE)[None, :] == full_owner, CAP, counts)
    return counts.astype(jnp.int32)


def draw_obs_cell(key, part):
    key = jax.random.fold_in(key, 12)
    key_level, key_row, key_col, key_pos = jax.random.split(key, 4)
    shape_all = (N_TILE, N_TILE, CAP)
    level_idx = jax.random.randint(key_level, shape_all, 0, LEV)
    row_idx = jax.random.randint(key_row, shape_all, 0, NY - 1)
    col_idx = jax.random.randint(key_col, shape_all, 0, CX - 1)
    cells = (level_idx * NY * CX + row_idx * CX + col_idx).reshape(-1)
    highest = (LEV - 1) * NY * CX + (NY - 2) * CX + CX - 2
    total_slots = N_TILE * N_TILE * CAP
    first_pos = jax.random.randint(key_pos, (), 0, total_slots)
    second_pos = (first_pos + 1) % total_slots
    cells = cells.at[first_pos].set(highest).at[second_pos].set(0)
    return cells.reshape(shape_all).astype(jnp.int32)


def block_scale(own_key, dims, pieces, low, top_value):
    def one(axis_at, parts):
        draws = jax.random.uniform(jax.random.fold_in(jax.random.fold_in(own_key, 6), axis_at), (parts,), jnp.float32, low / len(pieces), top_value / len(pieces))
        return jnp.repeat(jnp.exp(draws), dims[axis_at] // parts).reshape((-1,) + (1,) * (len(dims) - axis_at - 1))

    gain = one(*pieces[0])
    for cut in pieces[1:]:
        gain = gain * one(*cut)
    return gain


def normal_values(stream_key, extent, deviation, most, pieces=(), dtype=jnp.bfloat16):
    array = deviation * jax.random.normal(stream_key, extent, jnp.float32)
    if pieces:
        array = array * block_scale(stream_key, extent, pieces, -0.22, 0.18)
    return jnp.clip(array, -most, most).astype(dtype)


def setup_inputs(seed: int = 0) -> dict:
    seeds = jax.random.split(jax.random.key(seed), 8)
    return {
        "perturb": normal_values(seeds[0], (MEMBERS, LEV, NY, NX), 1.0, 6.0, ((0, 8), (3, 64))),
        "control": normal_values(seeds[1], (MEMBERS, LEV, NY, NX), 1.0, 6.0, ((0, 8), (3, 64)), jnp.float32),
        "obs_cell": draw_obs_cell(jax.random.fold_in(seeds[7], 71), 0),
        "obs_count": draw_obs_count(jax.random.fold_in(seeds[7], 71), 0),
        "obs_frac": jnp.clip(1.0 * jax.random.uniform(seeds[4], (N_TILE, 2, N_TILE, CAP), jnp.float32) ** block_scale(seeds[4], (N_TILE, 2, N_TILE, CAP), ((0, 64),), -0.2, 0.2), 0.0, 1.0),
        "obs_innov": normal_values(seeds[5], (N_TILE, N_TILE, CAP), 1.0, 6.0, ((0, 64),), jnp.float32),
        "obs_prec": jnp.clip(jnp.exp(math.log(10.0) - 2.3025851 * jax.random.uniform(seeds[6], (N_TILE, N_TILE, CAP), jnp.float32) ** block_scale(seeds[6], (N_TILE, N_TILE, CAP), ((0, 64),), -0.2, 0.2)), 1.0, 10.0),
    }


EXACT_MODE = lax.Precision.HIGHEST

def band_table(col_count):
    source_pos = jnp.arange(3 * col_count) - col_count
    target_pos = jnp.arange(col_count)
    offset = source_pos[:, None] - target_pos[None, :]
    distance = offset.astype(jnp.float32)
    weights = jnp.exp(-0.5 * distance * distance / (col_count * col_count))
    return jnp.where(jnp.abs(offset) <= col_count, weights, jnp.zeros_like(weights))

def row_table(row_count, scale):
    offset = (jnp.arange(row_count)[:, None] - jnp.arange(row_count)[None, :]).astype(jnp.float32)
    return jnp.exp(-0.5 * offset * offset / (scale * scale))

def norm_factor(col_count, row_count, scale):
    along_x = jnp.arange(-col_count, col_count + 1).astype(jnp.float32)
    along_y = jnp.arange(-(row_count - 1), row_count).astype(jnp.float32)
    total_x = jnp.sum(jnp.exp(-along_x * along_x / (col_count * col_count)))
    total_y = jnp.sum(jnp.exp(-along_y * along_y / (scale * scale)))
    return 1.0 / jnp.sqrt(total_x * total_y)

def localize(field, band, rowmat, factor):
    blocks = field.reshape(LEV, NY, N_TILE, CX)
    extended = jnp.concatenate([jnp.roll(blocks, 1, axis=2), blocks, jnp.roll(blocks, -1, axis=2)], axis=3)
    swept = jnp.einsum('lytk,kc->lytc', extended, band, precision=EXACT_MODE)
    mixed = jnp.einsum('iy,lytc->litc', rowmat, swept, precision=EXACT_MODE)
    return (factor * mixed).reshape(LEV, NY, N_TILE * CX)

def reference(perturb, control, obs_cell, obs_count, obs_frac, obs_innov, obs_prec):
    band = band_table(CX)
    rowmat = row_table(NY, YSCALE)
    factor = norm_factor(CX, NY, YSCALE)
    spread = 1.0 / math.sqrt(MEMBERS - 1)

    def accumulate(total, pair):
        member, alpha = pair
        return (total + member.astype(jnp.float32) * localize(alpha, band, rowmat, factor), None)
    summed, _ = lax.scan(accumulate, jnp.zeros((LEV, NY, NX), jnp.float32), (perturb, control))
    increment = spread * summed
    slot_ids = jnp.arange(CAP)[None, None, :]
    live_mask = (slot_ids < obs_count[:, :, None]).astype(jnp.float32)
    owners = jnp.broadcast_to(jnp.arange(N_TILE)[None, :, None], obs_cell.shape)
    level_idx = obs_cell // (NY * CX)
    inside = obs_cell % (NY * CX)
    row_idx = inside // CX
    col_idx = owners * CX + inside % CX
    frac_x = obs_frac[:, 0]
    frac_y = obs_frac[:, 1]
    weight_aa = (1.0 - frac_x) * (1.0 - frac_y)
    weight_ab = frac_x * (1.0 - frac_y)
    weight_ba = (1.0 - frac_x) * frac_y
    weight_bb = frac_x * frac_y
    value = weight_aa * increment[level_idx, row_idx, col_idx] + weight_ab * increment[level_idx, row_idx, col_idx + 1]
    value = value + weight_ba * increment[level_idx, row_idx + 1, col_idx]
    value = value + weight_bb * increment[level_idx, row_idx + 1, col_idx + 1]
    weighted = obs_prec * live_mask * (value - obs_innov)
    adjoint = jnp.zeros((LEV, NY, NX), jnp.float32)
    adjoint = adjoint.at[level_idx, row_idx, col_idx].add(weighted * weight_aa)
    adjoint = adjoint.at[level_idx, row_idx, col_idx + 1].add(weighted * weight_ab)
    adjoint = adjoint.at[level_idx, row_idx + 1, col_idx].add(weighted * weight_ba)
    adjoint = adjoint.at[level_idx, row_idx + 1, col_idx + 1].add(weighted * weight_bb)

    def member_grad(pair):
        member, alpha = pair
        return alpha + spread * localize(member.astype(jnp.float32) * adjoint, band, rowmat, factor)
    return lax.map(member_grad, (perturb, control))
```

```python
import math

import jax
import jax.numpy as jnp
import ml_dtypes
import numpy as np
from jax import lax
from jax.experimental import pallas as pl
from jax.experimental.pallas import tpu as pltpu
from jax.sharding import PartitionSpec as P

YSCALE = 1
F32 = jnp.float32
BF16 = jnp.bfloat16


def halves(table):
    high = table.astype(np.float32).astype(ml_dtypes.bfloat16)
    low = (table.astype(np.float32) - high.astype(np.float32)).astype(ml_dtypes.bfloat16)
    return high, low


def tables(col_count, row_count, scale, copies):
    offset = (np.arange(3 * col_count) - col_count)[:, None] - np.arange(col_count)[None, :]
    band = np.where(np.abs(offset) <= col_count, np.exp(-0.5 * (offset / col_count) ** 2), 0.0)
    row_offset = np.arange(row_count)[:, None] - np.arange(row_count)[None, :]
    rows = np.exp(-0.5 * (row_offset / scale) ** 2)
    along_x = np.arange(-col_count, col_count + 1)
    along_y = np.arange(-(row_count - 1), row_count)
    total = np.sum(np.exp(-((along_x / col_count) ** 2))) * np.sum(np.exp(-((along_y / scale) ** 2)))
    mixed = np.kron(np.eye(copies), rows) / np.sqrt(total)
    band_high, band_low = halves(band)
    mixed_high, mixed_low = halves(mixed)
    return (
        np.concatenate([band_high, band_high, band_low], axis=0),
        np.concatenate([mixed_high, mixed_high, mixed_low], axis=1),
    )


def split(values):
    high = values.astype(BF16)
    return high, (values - high.astype(F32)).astype(BF16)


def localize(extended, band, mixed):
    high, low = split(extended)
    swept = jnp.dot(jnp.concatenate([high, low, high], axis=1), band, preferred_element_type=F32)
    high, low = split(swept)
    return jnp.dot(mixed, jnp.concatenate([high, low, high], axis=0), preferred_element_type=F32)


def extend(even, own, near, far):
    left = jnp.where(even, far, near)
    right = jnp.where(even, near, far)
    return jnp.concatenate([left, own, right], axis=1)


def pack_kernel(cell_ref, count_ref, frac_ref, innov_ref, prec_ref, out_ref):
    tiles, slots = innov_ref.shape
    row = lax.broadcasted_iota(jnp.int32, (tiles, tiles), 0)
    col = lax.broadcasted_iota(jnp.int32, (tiles, tiles), 1)
    counts = jnp.where(row == col, jnp.broadcast_to(count_ref[...], (tiles, tiles)), 0)
    counts = jnp.sum(counts.astype(F32), axis=1, keepdims=True)
    slot = lax.broadcasted_iota(jnp.int32, (tiles, slots), 1).astype(F32)
    live = jnp.where(slot < counts, 1.0, 0.0)
    out_ref[...] = jnp.concatenate(
        [
            frac_ref[0],
            frac_ref[1],
            innov_ref[...],
            prec_ref[...] * live,
            cell_ref[...].astype(F32),
            jnp.zeros((tiles, 128 - 5 * slots), F32),
        ],
        axis=1,
    )


def partial_kernel(spread, even_ref, own_ref, near_ref, far_ref, perturb_ref, band_ref, mixed_ref, out_ref):
    even = even_ref[0] == 1
    rows = out_ref.shape[1]
    extended = extend(even, own_ref[...], near_ref[...], far_ref[...])
    localized = localize(extended, band_ref[...], mixed_ref[...])
    product = perturb_ref[...].astype(F32) * localized
    total = product[:rows]
    for start in range(rows, product.shape[0], rows):
        total = total + product[start : start + rows]
    total = spread * total
    for copy in range(out_ref.shape[0]):
        out_ref[copy] = total


def obs_kernel(slots, row_count, partial_ref, obs_ref, perturb_ref, out_ref):
    field = partial_ref[0]
    for member in range(1, partial_ref.shape[0]):
        field = field + partial_ref[member]
    rows, cols = field.shape
    turned = jnp.transpose(obs_ref[...])
    half = slots // 2

    def quantity(index):
        first = turned[index * slots : index * slots + half]
        second = turned[index * slots + half : (index + 1) * slots]
        return jnp.concatenate([first, second], axis=1)

    frac_x, frac_y, innov, prec, cell = (quantity(i) for i in range(5))
    cell = (cell + 0.5).astype(jnp.int32)
    corner_row = cell // cols
    corner_col = cell - corner_row * cols
    lanes = frac_x.shape[1]
    row_at = lax.broadcasted_iota(jnp.int32, (rows, lanes), 0)
    col_at = lax.broadcasted_iota(jnp.int32, (cols, lanes), 0)
    row_parts, col_parts = [], []
    for k in range(half):
        r, x = corner_row[k : k + 1], corner_col[k : k + 1]
        fy, fx = frac_y[k : k + 1], frac_x[k : k + 1]
        row_parts.append(jnp.where(row_at == r, 1.0 - fy, jnp.where(row_at == r + 1, fy, 0.0)))
        col_parts.append(jnp.where(col_at == x, 1.0 - fx, jnp.where(col_at == x + 1, fx, 0.0)))
    row_all = jnp.concatenate(row_parts, axis=1)
    row_high, row_low = split(row_all)
    field_high, field_low = split(jnp.transpose(field))
    picked = jnp.dot(
        jnp.concatenate([field_high, field_low, field_high], axis=1),
        jnp.concatenate([row_high, row_high, row_low], axis=0),
        preferred_element_type=F32,
    )
    weighted = []
    for k in range(half):
        value = jnp.sum(picked[:, k * lanes : (k + 1) * lanes] * col_parts[k], axis=0, keepdims=True)
        weighted.append(prec[k : k + 1] * (value - innov[k : k + 1]))
    weighted = jnp.concatenate(weighted, axis=1)
    rows_high, rows_low = split(row_all * weighted)
    cols_high, cols_low = split(jnp.concatenate(col_parts, axis=1))
    adjoint = lax.dot_general(
        jnp.concatenate([rows_high, rows_low, rows_high], axis=1),
        jnp.concatenate([cols_high, cols_high, cols_low], axis=1),
        (((1,), (1,)), ((), ())),
        preferred_element_type=F32,
    )
    for start in range(0, out_ref.shape[0], rows):
        out_ref[start : start + rows] = perturb_ref[start : start + rows].astype(F32) * adjoint


def final_kernel(spread, even_ref, control_ref, own_ref, near_ref, far_ref, band_ref, mixed_ref, out_ref):
    even = even_ref[0] == 1
    extended = extend(even, own_ref[...], near_ref[...], far_ref[...])
    out_ref[...] = control_ref[...] + spread * localize(extended, band_ref[...], mixed_ref[...])


def call(kernel, out_shape, scalars, arrays):
    specs = [pl.BlockSpec(memory_space=pltpu.SMEM)] * scalars + [pl.BlockSpec(memory_space=pltpu.VMEM)] * arrays
    return pl.pallas_call(
        kernel,
        out_shape=jax.ShapeDtypeStruct(out_shape, F32),
        in_specs=specs,
        out_specs=pl.BlockSpec(memory_space=pltpu.VMEM),
        compiler_params=pltpu.CompilerParams(vmem_limit_bytes=24 * 1024 * 1024),
    )


def per_device(perturb, control, obs_cell, obs_count, obs_frac, obs_innov, obs_prec):
    mem_local, levels, row_count, col_count = perturb.shape
    members = lax.axis_size("mem")
    tiles = lax.axis_size("tile")
    spread = 1.0 / math.sqrt(mem_local * members - 1)
    slots = obs_cell.shape[2]
    rows = levels * row_count
    band, mixed = tables(col_count, row_count, YSCALE, mem_local * levels)
    band, mixed = jnp.asarray(band), jnp.asarray(mixed)
    even = (1 - lax.axis_index("tile") % 2).astype(jnp.int32).reshape(1)
    near_pairs = [(i, i ^ 1) for i in range(tiles)]
    far_pairs = [(i, (i + 1) % tiles if i % 2 else (i - 1) % tiles) for i in range(tiles)]

    def neighbours(own):
        far = lax.ppermute(own, "tile", far_pairs)
        near = lax.ppermute(own, "tile", near_pairs)
        return near, far

    flat = mem_local * rows
    own = control.reshape(flat, col_count)
    weights = perturb.reshape(flat, col_count)

    near, far = neighbours(own)
    packed = call(pack_kernel, (tiles, 128), 0, 5)(
        obs_cell[0], obs_count, obs_frac[0], obs_innov[0], obs_prec[0]
    )
    arrived = lax.all_to_all(packed.reshape(tiles, 1, 128), "tile", split_axis=0, concat_axis=0, tiled=True)
    partials = call(lambda *refs: partial_kernel(spread, *refs), (members, rows, col_count), 1, 6)(
        even, own, near, far, weights, band, mixed
    )
    partials = lax.all_to_all(partials, "mem", split_axis=0, concat_axis=0, tiled=True)
    product = call(lambda *refs: obs_kernel(slots, row_count, *refs), (flat, col_count), 0, 3)(
        partials, arrived.reshape(tiles, 128), weights
    )
    near, far = neighbours(product)
    gradient = call(lambda *refs: final_kernel(spread, *refs), (flat, col_count), 1, 6)(
        even, own, product, near, far, band, mixed
    )
    return gradient.reshape(control.shape)


def solution(mesh):
    return jax.shard_map(
        per_device,
        mesh=mesh,
        in_specs=(
            P("mem", None, None, "tile"),
            P("mem", None, None, "tile"),
            P("tile", None, None),
            P("tile", None),
            P("tile", None, None, None),
            P("tile", None, None),
            P("tile", None, None),
        ),
        out_specs=P("mem", None, None, "tile"),
        check_vma=False,
    )
```

```python
import math

import jax
import jax.numpy as jnp
import ml_dtypes
import numpy as np
from jax import lax
from jax.experimental import pallas as pl
from jax.experimental.pallas import tpu as pltpu
from jax.sharding import PartitionSpec as P

YSCALE = 1
F32 = jnp.float32
BF16 = jnp.bfloat16


def halves(table):
    high = table.astype(np.float32).astype(ml_dtypes.bfloat16)
    low = (table.astype(np.float32) - high.astype(np.float32)).astype(ml_dtypes.bfloat16)
    return high, low


def tables(col_count, row_count, scale, levels):
    offset = (np.arange(3 * col_count) - col_count)[:, None] - np.arange(col_count)[None, :]
    band = np.where(np.abs(offset) <= col_count, np.exp(-0.5 * (offset / col_count) ** 2), 0.0)
    row_offset = np.arange(row_count)[:, None] - np.arange(row_count)[None, :]
    rows = np.exp(-0.5 * (row_offset / scale) ** 2)
    along_x = np.arange(-col_count, col_count + 1)
    along_y = np.arange(-(row_count - 1), row_count)
    total = np.sum(np.exp(-((along_x / col_count) ** 2))) * np.sum(np.exp(-((along_y / scale) ** 2)))
    mixed = np.kron(np.eye(levels), rows) / np.sqrt(total)
    band_high, band_low = halves(band)
    mixed_high, mixed_low = halves(mixed)
    mixed = np.concatenate([mixed_high, mixed_high, mixed_low], axis=1)
    mixed = np.pad(mixed, ((0, 0), (0, col_count - mixed.shape[1])))
    return np.concatenate([band_high, band_low, mixed], axis=0)


def split(values):
    high = values.astype(BF16)
    return high, (values - high.astype(F32)).astype(BF16)


def localize(extended, table_ref, rows):
    depth, cols = extended.shape[1], table_ref.shape[1]
    band_high, band_low = table_ref[:depth], table_ref[depth : 2 * depth]
    mixed = table_ref[2 * depth :, : 3 * rows]
    high, low = split(extended)
    swept = jnp.dot(
        jnp.concatenate([high, low, high], axis=1),
        jnp.concatenate([band_high, band_high, band_low], axis=0),
        preferred_element_type=F32,
    )
    swept = jnp.concatenate([swept[start : start + rows] for start in range(0, swept.shape[0], rows)], axis=1)
    high, low = split(swept)
    return jnp.dot(mixed, jnp.concatenate([high, low, high], axis=0), preferred_element_type=F32)


def extend(even, own, near, far):
    left = jnp.where(even, far, near)
    right = jnp.where(even, near, far)
    return jnp.concatenate([left, own, right], axis=1)


def pack_kernel(cell_ref, count_ref, frac_ref, innov_ref, prec_ref, out_ref):
    slots, tiles = innov_ref.shape
    cols = out_ref.shape[1]
    slot = lax.broadcasted_iota(jnp.int32, (slots, tiles), 0)
    live = jnp.where(slot < count_ref[...], 1.0, 0.0)
    cell = cell_ref[...]
    corner_row = cell // cols
    corner_col = cell - corner_row * cols
    packed = jnp.concatenate(
        [
            corner_col.astype(F32) + frac_ref[0],
            corner_row.astype(F32) + frac_ref[1],
            innov_ref[...],
            prec_ref[...] * live,
            jnp.zeros((out_ref.shape[1] - 4 * slots, tiles), F32),
        ],
        axis=0,
    )
    out_ref[...] = jnp.transpose(packed)


def partial_kernel(
    spread, slots, place_ref, own_ref, near_ref, far_ref, perturb_ref, obs_ref, table_ref, out_ref
):
    even = place_ref[0] == 1
    copies, cols = out_ref.shape[0], out_ref.shape[2]
    rows = table_ref.shape[0] - 6 * cols
    extended = extend(even, own_ref[...], near_ref[...], far_ref[...])
    localized = localize(extended, table_ref, rows)
    total = jnp.zeros((rows, cols), F32)
    for member in range(own_ref.shape[0] // rows):
        weights = perturb_ref[member * rows : (member + 1) * rows].astype(F32)
        total = total + weights * localized[:, member * cols : (member + 1) * cols]
    total = spread * total
    for copy in range(copies):
        out_ref[copy, :rows] = total

    @pl.when(place_ref[1] == 0)
    def _():
        turned = jnp.transpose(obs_ref[...])
        half = slots // 2
        for index in range(4):
            first = turned[index * slots : index * slots + half]
            second = turned[index * slots + half : (index + 1) * slots]
            quantity = jnp.concatenate([first, second], axis=1)
            for copy in range(copies):
                out_ref[copy, rows + index * half : rows + (index + 1) * half] = quantity

    @pl.when(place_ref[1] != 0)
    def _():
        for copy in range(copies):
            out_ref[copy, rows:] = jnp.zeros((out_ref.shape[1] - rows, cols), F32)


def obs_kernel(half, partial_ref, perturb_ref, out_ref):
    rows = partial_ref.shape[1] - 4 * half
    field = partial_ref[0, :rows]
    for member in range(1, partial_ref.shape[0]):
        field = field + partial_ref[member, :rows]
    cols = field.shape[1]
    at_x, at_y, innov, prec = (partial_ref[0, rows + i * half : rows + (i + 1) * half] for i in range(4))
    corner_col, corner_row = at_x.astype(jnp.int32), at_y.astype(jnp.int32)
    frac_x, frac_y = at_x - corner_col.astype(F32), at_y - corner_row.astype(F32)
    lanes = at_x.shape[1]
    row_at = lax.broadcasted_iota(jnp.int32, (rows, lanes), 0)
    col_at = lax.broadcasted_iota(jnp.int32, (cols, lanes), 0)
    row_parts, col_parts = [], []
    for k in range(half):
        r, x = corner_row[k : k + 1], corner_col[k : k + 1]
        fy, fx = frac_y[k : k + 1], frac_x[k : k + 1]
        row_parts.append(jnp.where(row_at == r, 1.0 - fy, jnp.where(row_at == r + 1, fy, 0.0)))
        col_parts.append(jnp.where(col_at == x, 1.0 - fx, jnp.where(col_at == x + 1, fx, 0.0)))
    row_all = jnp.concatenate(row_parts, axis=1)
    row_high, row_low = split(row_all)
    field_high, field_low = split(jnp.transpose(field))
    picked = jnp.dot(
        jnp.concatenate([field_high, field_low, field_high], axis=1),
        jnp.concatenate([row_high, row_high, row_low], axis=0),
        preferred_element_type=F32,
    )
    weighted = []
    for k in range(half):
        value = jnp.sum(picked[:, k * lanes : (k + 1) * lanes] * col_parts[k], axis=0, keepdims=True)
        weighted.append(prec[k : k + 1] * (value - innov[k : k + 1]))
    weighted = jnp.concatenate(weighted, axis=1)
    rows_high, rows_low = split(row_all * weighted)
    cols_high, cols_low = split(jnp.concatenate(col_parts, axis=1))
    adjoint = lax.dot_general(
        jnp.concatenate([rows_high, rows_low, rows_high], axis=1),
        jnp.concatenate([cols_high, cols_high, cols_low], axis=1),
        (((1,), (1,)), ((), ())),
        preferred_element_type=F32,
    )
    for start in range(0, out_ref.shape[0], rows):
        out_ref[start : start + rows] = perturb_ref[start : start + rows].astype(F32) * adjoint


def final_kernel(spread, place_ref, control_ref, own_ref, near_ref, far_ref, table_ref, out_ref):
    even = place_ref[0] == 1
    cols = out_ref.shape[1]
    rows = table_ref.shape[0] - 6 * cols
    extended = extend(even, own_ref[...], near_ref[...], far_ref[...])
    localized = localize(extended, table_ref, rows)
    for member in range(out_ref.shape[0] // rows):
        part = slice(member * rows, (member + 1) * rows)
        out_ref[part] = control_ref[part] + spread * localized[:, member * cols : (member + 1) * cols]


def call(kernel, out_shape, scalars, arrays):
    specs = [pl.BlockSpec(memory_space=pltpu.SMEM)] * scalars + [pl.BlockSpec(memory_space=pltpu.VMEM)] * arrays
    return pl.pallas_call(
        kernel,
        out_shape=jax.ShapeDtypeStruct(out_shape, F32),
        in_specs=specs,
        out_specs=pl.BlockSpec(memory_space=pltpu.VMEM),
        compiler_params=pltpu.CompilerParams(vmem_limit_bytes=24 * 1024 * 1024),
    )


def per_device(perturb, control, obs_cell, obs_count, obs_frac, obs_innov, obs_prec):
    mem_local, levels, row_count, col_count = perturb.shape
    members = lax.axis_size("mem")
    tiles = lax.axis_size("tile")
    spread = 1.0 / math.sqrt(mem_local * members - 1)
    slots = obs_cell.shape[2]
    rows = levels * row_count
    table = jnp.asarray(tables(col_count, row_count, YSCALE, levels))
    even = 1 - lax.axis_index("tile") % 2
    plane = lax.axis_index("mem")
    place = jnp.stack([even, plane]).astype(jnp.int32)
    near_pairs = [(i, i ^ 1) for i in range(tiles)]
    far_pairs = [(i, (i + 1) % tiles if i % 2 else (i - 1) % tiles) for i in range(tiles)]

    def neighbours(own):
        far = lax.ppermute(own, "tile", far_pairs)
        near = lax.ppermute(own, "tile", near_pairs)
        return near, far

    def route(cell, count, frac, innov, prec):
        packed = call(pack_kernel, (tiles, col_count), 0, 5)(
            cell[0].T, count, frac[0].transpose(0, 2, 1), innov[0].T, prec[0].T
        )
        packed = packed.reshape(tiles, 1, col_count)
        arrived = lax.all_to_all(packed, "tile", split_axis=0, concat_axis=0, tiled=True)
        return arrived.reshape(tiles, col_count)

    def skip(cell, count, frac, innov, prec):
        return jnp.zeros((tiles, col_count), F32)

    flat = mem_local * rows
    own = control.reshape(flat, col_count)
    weights = perturb.reshape(flat, col_count)

    near, far = neighbours(own)
    arrived = lax.cond(plane == 0, route, skip, obs_cell, obs_count, obs_frac, obs_innov, obs_prec)
    partials = call(lambda *refs: partial_kernel(spread, slots, *refs), (members, rows + 2 * slots, col_count), 1, 6)(
        place, own, near, far, weights, arrived, table
    )
    partials = lax.all_to_all(partials, "mem", split_axis=0, concat_axis=0, tiled=True)
    product = call(lambda *refs: obs_kernel(slots // 2, *refs), (flat, col_count), 0, 2)(partials, weights)
    near, far = neighbours(product)
    gradient = call(lambda *refs: final_kernel(spread, *refs), (flat, col_count), 1, 5)(
        place, own, product, near, far, table
    )
    return gradient.reshape(control.shape)


def solution(mesh):
    return jax.shard_map(
        per_device,
        mesh=mesh,
        in_specs=(
            P("mem", None, None, "tile"),
            P("mem", None, None, "tile"),
            P("tile", None, None),
            P("tile", None),
            P("tile", None, None, None),
            P("tile", None, None),
            P("tile", None, None),
        ),
        out_specs=P("mem", None, None, "tile"),
        check_vma=False,
    )
```

```python
import math

import jax
import jax.numpy as jnp
import ml_dtypes
import numpy as np
from jax import lax
from jax.experimental import pallas as pl
from jax.experimental.pallas import tpu as pltpu
from jax.sharding import PartitionSpec as P

YSCALE = 1
F32 = jnp.float32
BF16 = jnp.bfloat16
ROUTING_PLANE = 1
MEMBER_LEAD = 6
TILE_LEAD = 40


def halves(table):
    high = table.astype(np.float32).astype(ml_dtypes.bfloat16)
    low = (table.astype(np.float32) - high.astype(np.float32)).astype(ml_dtypes.bfloat16)
    return high, low


def tables(col_count, row_count, scale, levels):
    offset = (np.arange(3 * col_count) - col_count)[:, None] - np.arange(col_count)[None, :]
    band = np.where(np.abs(offset) <= col_count, np.exp(-0.5 * (offset / col_count) ** 2), 0.0)
    row_offset = np.arange(row_count)[:, None] - np.arange(row_count)[None, :]
    rows = np.exp(-0.5 * (row_offset / scale) ** 2)
    along_x = np.arange(-col_count, col_count + 1)
    along_y = np.arange(-(row_count - 1), row_count)
    total = np.sum(np.exp(-((along_x / col_count) ** 2))) * np.sum(np.exp(-((along_y / scale) ** 2)))
    mixed = np.kron(np.eye(levels), rows) / np.sqrt(total)
    mixed = np.tile(mixed, (1, col_count // mixed.shape[1]))
    return np.concatenate([*halves(band), *halves(mixed)], axis=0)


def split(values):
    high = values.astype(BF16)
    return high, (values - high.astype(F32)).astype(BF16)


def localize(extended, table_ref, rows):
    flat, depth = extended.shape
    cols = table_ref.shape[1]
    row_block = lax.broadcasted_iota(jnp.int32, (flat, flat), 0) // rows
    same = row_block == lax.broadcasted_iota(jnp.int32, (flat, flat), 1) // rows

    def mixing(start):
        strip = table_ref[start : start + rows].astype(F32)
        strip = jnp.concatenate([strip] * pl.cdiv(flat, cols), axis=1)[:, :flat]
        return jnp.where(same, jnp.concatenate([strip] * (flat // rows), axis=0), 0.0).astype(BF16)

    mixed_high, mixed_low = mixing(2 * depth), mixing(2 * depth + rows)
    band_high, band_low = table_ref[:depth], table_ref[depth : 2 * depth]
    high, low = split(extended)
    swept = jnp.dot(
        jnp.concatenate([high, low, high], axis=1),
        jnp.concatenate([band_high, band_high, band_low], axis=0),
        preferred_element_type=F32,
    )
    high, low = split(swept)
    both = jnp.dot(mixed_high, jnp.concatenate([high, low], axis=1), preferred_element_type=F32)
    return both[:, :cols] + both[:, cols:] + jnp.dot(mixed_low, high, preferred_element_type=F32)


def extend(even, own, near, far):
    left = jnp.where(even, far, near)
    right = jnp.where(even, near, far)
    return jnp.concatenate([left, own, right], axis=1)


def pack_kernel(lead, cell_ref, count_ref, frac_ref, innov_ref, prec_ref, out_ref):
    slots, tiles = innov_ref.shape
    cols = out_ref.shape[1]
    slot = lax.broadcasted_iota(jnp.int32, (slots, tiles), 0)
    live = jnp.where(slot < count_ref[...], 1.0, 0.0)
    cell = cell_ref[...]
    corner_row = cell // cols
    corner_col = cell - corner_row * cols
    packed = jnp.concatenate(
        [
            corner_col.astype(F32) + frac_ref[0],
            corner_row.astype(F32) + frac_ref[1],
            innov_ref[...],
            prec_ref[...] * live,
            jnp.zeros((out_ref.shape[1] - 4 * slots, tiles), F32),
        ],
        axis=0,
    )
    turned = jnp.transpose(packed)
    out_ref[: tiles - lead] = turned[lead:]
    out_ref[tiles - lead :] = turned[:lead]


def partial_sum(spread, rows, even, own_ref, near_ref, far_ref, perturb_ref, table_ref):
    extended = extend(even, own_ref[...], near_ref[...], far_ref[...])
    product = perturb_ref[...].astype(F32) * localize(extended, table_ref, rows)
    total = product[:rows]
    for start in range(rows, product.shape[0], rows):
        total = total + product[start : start + rows]
    return spread * total


def partial_kernel(spread, even_ref, own_ref, near_ref, far_ref, perturb_ref, table_ref, out_ref):
    even = even_ref[0] == 1
    out_ref[...] = partial_sum(spread, out_ref.shape[0], even, own_ref, near_ref, far_ref, perturb_ref, table_ref)


def partial_copies_kernel(spread, rows, even_ref, own_ref, near_ref, far_ref, perturb_ref, table_ref, out_ref):
    even = even_ref[0] == 1
    total = partial_sum(spread, rows, even, own_ref, near_ref, far_ref, perturb_ref, table_ref)
    for copy in range(out_ref.shape[0]):
        out_ref[copy, :rows] = total
        out_ref[copy, rows:] = jnp.zeros((out_ref.shape[1] - rows, out_ref.shape[2]), F32)


def join_kernel(slots, partial_ref, obs_ref, out_ref):
    rows = partial_ref.shape[0]
    total = partial_ref[...]
    turned = jnp.transpose(obs_ref[...])
    half = slots // 2
    quantities = []
    for index in range(4):
        first = turned[index * slots : index * slots + half]
        second = turned[index * slots + half : (index + 1) * slots]
        quantities.append(jnp.concatenate([first, second], axis=1))
    for copy in range(out_ref.shape[0]):
        out_ref[copy, :rows] = total
        for index, quantity in enumerate(quantities):
            out_ref[copy, rows + index * half : rows + (index + 1) * half] = quantity


def obs_kernel(half, source, partial_ref, perturb_ref, out_ref):
    rows = partial_ref.shape[1] - 4 * half
    field = partial_ref[0, :rows]
    for member in range(1, partial_ref.shape[0]):
        field = field + partial_ref[member, :rows]
    cols = field.shape[1]
    at_x, at_y, innov, prec = (partial_ref[source, rows + i * half : rows + (i + 1) * half] for i in range(4))
    corner_col, corner_row = at_x.astype(jnp.int32), at_y.astype(jnp.int32)
    frac_x, frac_y = at_x - corner_col.astype(F32), at_y - corner_row.astype(F32)
    lanes = at_x.shape[1]
    row_at = lax.broadcasted_iota(jnp.int32, (rows, lanes), 0)
    col_at = lax.broadcasted_iota(jnp.int32, (cols, lanes), 0)
    row_parts, col_parts = [], []
    for k in range(half):
        r, x = corner_row[k : k + 1], corner_col[k : k + 1]
        fy, fx = frac_y[k : k + 1], frac_x[k : k + 1]
        row_parts.append(jnp.where(row_at == r, 1.0 - fy, jnp.where(row_at == r + 1, fy, 0.0)))
        col_parts.append(jnp.where(col_at == x, 1.0 - fx, jnp.where(col_at == x + 1, fx, 0.0)))
    row_all = jnp.concatenate(row_parts, axis=1)
    row_high, row_low = split(row_all)
    field_high, field_low = split(jnp.transpose(field))
    picked = jnp.dot(
        jnp.concatenate([field_high, field_low, field_high], axis=1),
        jnp.concatenate([row_high, row_high, row_low], axis=0),
        preferred_element_type=F32,
    )
    weighted = []
    for k in range(half):
        value = jnp.sum(picked[:, k * lanes : (k + 1) * lanes] * col_parts[k], axis=0, keepdims=True)
        weighted.append(prec[k : k + 1] * (value - innov[k : k + 1]))
    weighted = jnp.concatenate(weighted, axis=1)
    rows_high, rows_low = split(row_all * weighted)
    cols_high, cols_low = split(jnp.concatenate(col_parts, axis=1))
    adjoint = lax.dot_general(
        jnp.concatenate([rows_high, rows_low, rows_high], axis=1),
        jnp.concatenate([cols_high, cols_high, cols_low], axis=1),
        (((1,), (1,)), ((), ())),
        preferred_element_type=F32,
    )
    for start in range(0, out_ref.shape[0], rows):
        out_ref[start : start + rows] = perturb_ref[start : start + rows].astype(F32) * adjoint


def final_kernel(spread, rows, even_ref, control_ref, own_ref, near_ref, far_ref, table_ref, out_ref):
    even = even_ref[0] == 1
    extended = extend(even, own_ref[...], near_ref[...], far_ref[...])
    out_ref[...] = control_ref[...] + spread * localize(extended, table_ref, rows)


def call(kernel, out_shape, scalars, arrays):
    specs = [pl.BlockSpec(memory_space=pltpu.SMEM)] * scalars + [pl.BlockSpec(memory_space=pltpu.VMEM)] * arrays
    return pl.pallas_call(
        kernel,
        out_shape=jax.ShapeDtypeStruct(out_shape, F32),
        in_specs=specs,
        out_specs=pl.BlockSpec(memory_space=pltpu.VMEM),
        compiler_params=pltpu.CompilerParams(vmem_limit_bytes=24 * 1024 * 1024),
    )


def per_device(perturb, control, obs_cell, obs_count, obs_frac, obs_innov, obs_prec):
    mem_local, levels, row_count, col_count = perturb.shape
    members = lax.axis_size("mem")
    tiles = lax.axis_size("tile")
    spread = 1.0 / math.sqrt(mem_local * members - 1)
    slots = obs_cell.shape[2]
    rows = levels * row_count
    table = jnp.asarray(tables(col_count, row_count, YSCALE, levels))
    even = (1 - lax.axis_index("tile") % 2).astype(jnp.int32).reshape(1)
    tile_lead = TILE_LEAD
    tile_order = [[(i + tile_lead) % tiles for i in range(tiles)]]
    member_order = [[(i + MEMBER_LEAD) % members for i in range(members)]]
    near_pairs = [(i, i ^ 1) for i in range(tiles)]
    far_pairs = [(i, (i + 1) % tiles if i % 2 else (i - 1) % tiles) for i in range(tiles)]

    def neighbours(own):
        far = lax.ppermute(own, "tile", far_pairs)
        near = lax.ppermute(own, "tile", near_pairs)
        return near, far

    flat = mem_local * rows
    joined = (members, rows + 2 * slots, col_count)

    def route(even, own, weights, table, cell, count, frac, innov, prec):
        packed = call(lambda *refs: pack_kernel(tile_lead, *refs), (tiles, col_count), 0, 5)(
            cell[0].T, count, frac[0].transpose(0, 2, 1), innov[0].T, prec[0].T
        )
        packed = packed.reshape(tiles, 1, col_count)
        arrived = lax.all_to_all(
            packed, "tile", split_axis=0, concat_axis=0, tiled=True, axis_index_groups=tile_order
        )
        near, far = neighbours(own)
        partial = call(lambda *refs: partial_kernel(spread, *refs), (rows, col_count), 1, 5)(
            even, own, near, far, weights, table
        )
        return call(lambda *refs: join_kernel(slots, *refs), joined, 0, 2)(partial, arrived.reshape(tiles, col_count))

    def plain(even, own, weights, table, cell, count, frac, innov, prec):
        near, far = neighbours(own)
        return call(lambda *refs: partial_copies_kernel(spread, rows, *refs), joined, 1, 5)(
            even, own, near, far, weights, table
        )

    own = control.reshape(flat, col_count)
    weights = perturb.reshape(flat, col_count)
    partials = lax.cond(
        lax.axis_index("mem") == ROUTING_PLANE,
        route,
        plain,
        *(even, own, weights, table, obs_cell, obs_count, obs_frac, obs_innov, obs_prec),
    )
    partials = lax.all_to_all(
        partials, "mem", split_axis=0, concat_axis=0, tiled=True, axis_index_groups=member_order
    )
    source = (ROUTING_PLANE - MEMBER_LEAD) % members
    product = call(lambda *refs: obs_kernel(slots // 2, source, *refs), (flat, col_count), 0, 2)(partials, weights)
    near, far = neighbours(product)
    gradient = call(lambda *refs: final_kernel(spread, rows, *refs), (flat, col_count), 1, 5)(
        even, own, product, near, far, table
    )
    return gradient.reshape(control.shape)


def solution(mesh):
    return jax.shard_map(
        per_device,
        mesh=mesh,
        in_specs=(
            P("mem", None, None, "tile"),
            P("mem", None, None, "tile"),
            P("tile", None, None),
            P("tile", None),
            P("tile", None, None, None),
            P("tile", None, None),
            P("tile", None, None),
        ),
        out_specs=P("mem", None, None, "tile"),
        check_vma=False,
    )
```

```python
import math

import jax
import jax.numpy as jnp
import ml_dtypes
import numpy as np
from jax import lax
from jax.experimental import pallas as pl
from jax.experimental.pallas import tpu as pltpu
from jax.sharding import PartitionSpec as P

YSCALE = 1
F32 = jnp.float32
BF16 = jnp.bfloat16
ROUTING_PLANES = (0, 1)
TILE_BLOCKS = (5, 6, 7, 0, 1, 2, 3, 4)
MEMBER_ORDER = (7, 6, 5, 4, 3, 2, 1, 0)


def halves(table):
    high = table.astype(np.float32).astype(ml_dtypes.bfloat16)
    low = (table.astype(np.float32) - high.astype(np.float32)).astype(ml_dtypes.bfloat16)
    return high, low


def tables(col_count, row_count, scale, levels):
    offset = (np.arange(3 * col_count) - col_count)[:, None] - np.arange(col_count)[None, :]
    band = np.where(np.abs(offset) <= col_count, np.exp(-0.5 * (offset / col_count) ** 2), 0.0)
    row_offset = np.arange(row_count)[:, None] - np.arange(row_count)[None, :]
    rows = np.exp(-0.5 * (row_offset / scale) ** 2)
    along_x = np.arange(-col_count, col_count + 1)
    along_y = np.arange(-(row_count - 1), row_count)
    total = np.sum(np.exp(-((along_x / col_count) ** 2))) * np.sum(np.exp(-((along_y / scale) ** 2)))
    mixed = np.kron(np.eye(levels), rows) / np.sqrt(total)
    mixed = np.tile(mixed, (1, col_count // mixed.shape[1]))
    return np.concatenate([*halves(band), *halves(mixed)], axis=0)


def split(values):
    high = values.astype(BF16)
    return high, (values - high.astype(F32)).astype(BF16)


def localize(extended, table_ref, rows):
    flat, depth = extended.shape
    cols = table_ref.shape[1]
    row_block = lax.broadcasted_iota(jnp.int32, (flat, flat), 0) // rows
    same = row_block == lax.broadcasted_iota(jnp.int32, (flat, flat), 1) // rows

    def mixing(start):
        strip = table_ref[start : start + rows].astype(F32)
        strip = jnp.concatenate([strip] * pl.cdiv(flat, cols), axis=1)[:, :flat]
        return jnp.where(same, jnp.concatenate([strip] * (flat // rows), axis=0), 0.0).astype(BF16)

    mixed_high, mixed_low = mixing(2 * depth), mixing(2 * depth + rows)
    band_high, band_low = table_ref[:depth], table_ref[depth : 2 * depth]
    high, low = split(extended)
    swept = jnp.dot(
        jnp.concatenate([high, low, high], axis=1),
        jnp.concatenate([band_high, band_high, band_low], axis=0),
        preferred_element_type=F32,
    )
    high, low = split(swept)
    both = jnp.dot(mixed_high, jnp.concatenate([high, low], axis=1), preferred_element_type=F32)
    return both[:, :cols] + both[:, cols:] + jnp.dot(mixed_low, high, preferred_element_type=F32)


def extend(even, own, near, far):
    left = jnp.where(even, far, near)
    right = jnp.where(even, near, far)
    return jnp.concatenate([left, own, right], axis=1)


def pack_kernel(blocks, part_ref, cell_ref, count_ref, frac_ref, innov_ref, prec_ref, out_ref):
    tiles = innov_ref.shape[1]
    slots = innov_ref.shape[0] // len(ROUTING_PLANES)
    cols = out_ref.shape[1]
    start = pl.multiple_of(part_ref[0] * slots, slots)
    mine = pl.ds(start, slots)
    slot = start + lax.broadcasted_iota(jnp.int32, (slots, tiles), 0)
    live = jnp.where(slot < count_ref[...], 1.0, 0.0)
    cell = cell_ref[mine]
    corner_row = lax.shift_right_logical(cell, int(math.log2(cols)))
    corner_col = lax.bitwise_and(cell, cols - 1)
    packed = jnp.concatenate(
        [
            corner_col.astype(F32) + frac_ref[0, mine],
            corner_row.astype(F32) + frac_ref[1, mine],
            innov_ref[mine],
            prec_ref[mine] * live,
            jnp.zeros((out_ref.shape[1] - 4 * slots, tiles), F32),
        ],
        axis=0,
    )
    turned = jnp.transpose(packed)
    size = tiles // len(blocks)
    for place, block in enumerate(blocks):
        out_ref[place * size : (place + 1) * size] = turned[block * size : (block + 1) * size]


def partial_sum(spread, rows, even, own_ref, near_ref, far_ref, perturb_ref, table_ref):
    extended = extend(even, own_ref[...], near_ref[...], far_ref[...])
    product = perturb_ref[...].astype(F32) * localize(extended, table_ref, rows)
    total = product[:rows]
    for start in range(rows, product.shape[0], rows):
        total = total + product[start : start + rows]
    return spread * total


def partial_kernel(spread, even_ref, own_ref, near_ref, far_ref, perturb_ref, table_ref, out_ref, kept_ref):
    even = even_ref[0] == 1
    kept_ref[...] = perturb_ref[...]
    out_ref[...] = partial_sum(spread, out_ref.shape[0], even, own_ref, near_ref, far_ref, perturb_ref, table_ref)


def partial_copies_kernel(
    spread, rows, even_ref, own_ref, near_ref, far_ref, perturb_ref, table_ref, out_ref, kept_ref
):
    even = even_ref[0] == 1
    kept_ref[...] = perturb_ref[...]
    total = partial_sum(spread, rows, even, own_ref, near_ref, far_ref, perturb_ref, table_ref)
    for copy in range(out_ref.shape[0]):
        out_ref[copy, :rows] = total
        out_ref[copy, rows:] = jnp.zeros((out_ref.shape[1] - rows, out_ref.shape[2]), F32)


def join_kernel(partial_ref, obs_ref, out_ref):
    rows = partial_ref.shape[0]
    slots = (out_ref.shape[1] - rows) // 2
    total = partial_ref[...]
    turned = jnp.transpose(obs_ref[...])
    places = jnp.concatenate([turned[:slots], turned[slots : 2 * slots]], axis=1)
    values = jnp.concatenate([turned[2 * slots : 3 * slots], turned[3 * slots : 4 * slots]], axis=1)
    for copy in range(out_ref.shape[0]):
        out_ref[copy, :rows] = total
        out_ref[copy, rows : rows + slots] = places
        out_ref[copy, rows + slots :] = values


def obs_kernel(half, sources, partial_ref, perturb_ref, out_ref):
    rows = partial_ref.shape[1] - 2 * half
    field = partial_ref[0, :rows]
    for member in range(1, partial_ref.shape[0]):
        field = field + partial_ref[member, :rows]
    cols = field.shape[1]
    tiles = cols // 2

    def quantity(start, lane):
        parts = [partial_ref[source, rows + start : rows + start + half] for source in sources]
        return jnp.concatenate([part[:, lane : lane + tiles] for part in parts], axis=1)

    at_x, at_y, innov, prec = quantity(0, 0), quantity(0, tiles), quantity(half, 0), quantity(half, tiles)
    corner_col, corner_row = at_x.astype(jnp.int32), at_y.astype(jnp.int32)
    frac_x, frac_y = at_x - corner_col.astype(F32), at_y - corner_row.astype(F32)
    lanes = at_x.shape[1]
    row_at = lax.broadcasted_iota(jnp.int32, (rows, lanes), 0)
    col_at = lax.broadcasted_iota(jnp.int32, (cols, lanes), 0)
    row_parts, col_parts = [], []
    for k in range(half):
        r, x = corner_row[k : k + 1], corner_col[k : k + 1]
        fy, fx = frac_y[k : k + 1], frac_x[k : k + 1]
        row_parts.append(jnp.where(row_at == r, 1.0 - fy, jnp.where(row_at == r + 1, fy, 0.0)))
        col_parts.append(jnp.where(col_at == x, 1.0 - fx, jnp.where(col_at == x + 1, fx, 0.0)))
    row_all = jnp.concatenate(row_parts, axis=1)
    row_high, row_low = split(row_all)
    field_high, field_low = split(jnp.transpose(field))
    picked = jnp.dot(
        jnp.concatenate([field_high, field_low, field_high], axis=1),
        jnp.concatenate([row_high, row_high, row_low], axis=0),
        preferred_element_type=F32,
    )
    weighted = []
    for k in range(half):
        value = jnp.sum(picked[:, k * lanes : (k + 1) * lanes] * col_parts[k], axis=0, keepdims=True)
        weighted.append(prec[k : k + 1] * (value - innov[k : k + 1]))
    weighted = jnp.concatenate(weighted, axis=1)
    rows_high, rows_low = split(row_all * weighted)
    cols_high, cols_low = split(jnp.concatenate(col_parts, axis=1))
    adjoint = lax.dot_general(
        jnp.concatenate([rows_high, rows_low, rows_high], axis=1),
        jnp.concatenate([cols_high, cols_high, cols_low], axis=1),
        (((1,), (1,)), ((), ())),
        preferred_element_type=F32,
    )
    for start in range(0, out_ref.shape[0], rows):
        out_ref[start : start + rows] = perturb_ref[start : start + rows].astype(F32) * adjoint


def final_kernel(spread, rows, even_ref, control_ref, own_ref, near_ref, far_ref, table_ref, out_ref):
    even = even_ref[0] == 1
    extended = extend(even, own_ref[...], near_ref[...], far_ref[...])
    out_ref[...] = control_ref[...] + spread * localize(extended, table_ref, rows)


def call(kernel, out_shapes, scalars, arrays, flops=None):
    specs = [pl.BlockSpec(memory_space=pltpu.SMEM)] * scalars + [pl.BlockSpec(memory_space=pltpu.VMEM)] * arrays
    outs = [jax.ShapeDtypeStruct(shape, dtype) for shape, dtype in out_shapes]
    return pl.pallas_call(
        kernel,
        out_shape=outs,
        in_specs=specs,
        out_specs=[pl.BlockSpec(memory_space=pltpu.VMEM)] * len(outs),
        compiler_params=pltpu.CompilerParams(vmem_limit_bytes=24 * 1024 * 1024),
        cost_estimate=flops and pl.CostEstimate(flops=flops, bytes_accessed=0, transcendentals=0),
    )


def in_hbm(array):
    return pltpu.with_memory_space_constraint(array, pltpu.HBM)


def per_device(perturb, control, obs_cell, obs_count, obs_frac, obs_innov, obs_prec):
    mem_local, levels, row_count, col_count = perturb.shape
    members = lax.axis_size("mem")
    tiles = lax.axis_size("tile")
    spread = 1.0 / math.sqrt(mem_local * members - 1)
    slots = obs_cell.shape[2]
    rows = levels * row_count
    table = jnp.asarray(tables(col_count, row_count, YSCALE, levels))
    even = (1 - lax.axis_index("tile") % 2).astype(jnp.int32).reshape(1)
    size = tiles // len(TILE_BLOCKS)
    tile_order = [[block * size + i for block in TILE_BLOCKS for i in range(size)]]
    member_order = [list(MEMBER_ORDER)]
    near_pairs = [(i, i ^ 1) for i in range(tiles)]
    far_pairs = [(i, (i + 1) % tiles if i % 2 else (i - 1) % tiles) for i in range(tiles)]

    def neighbours(own):
        far = lax.ppermute(own, "tile", far_pairs)
        near = lax.ppermute(own, "tile", near_pairs)
        return near, far

    flat = mem_local * rows
    half = slots // len(ROUTING_PLANES)
    joined = (members, rows + 2 * half, col_count)

    kept = ((flat, col_count), BF16)

    def route(part, even, own, weights, table, cell, count, frac, innov, prec):
        obs = (cell[0].T, count, frac[0].transpose(0, 2, 1), innov[0].T, prec[0].T)
        pack = call(lambda *refs: pack_kernel(TILE_BLOCKS, *refs), [((tiles, col_count), F32)], 1, 5, 10**9)
        (packed,) = pack(part, *map(in_hbm, obs))
        packed = packed.reshape(tiles, 1, col_count)
        arrived = lax.all_to_all(
            packed, "tile", split_axis=0, concat_axis=0, tiled=True, axis_index_groups=tile_order
        )
        near, far = neighbours(own)
        summing = call(lambda *refs: partial_kernel(spread, *refs), [((rows, col_count), F32), kept], 1, 5, 1000)
        partial, weights = summing(even, own, near, far, in_hbm(weights), table)
        (partials,) = call(join_kernel, [(joined, F32)], 0, 2)(partial, arrived.reshape(tiles, col_count))
        return partials, weights

    def plain(part, even, own, weights, table, cell, count, frac, innov, prec):
        near, far = neighbours(own)
        summing = call(lambda *refs: partial_copies_kernel(spread, rows, *refs), [(joined, F32), kept], 1, 5)
        return tuple(summing(even, own, near, far, in_hbm(weights), table))

    own = control.reshape(flat, col_count)
    weights = perturb.reshape(flat, col_count)
    part = (lax.axis_index("mem") - ROUTING_PLANES[0]).astype(jnp.int32).reshape(1)
    partials, weights = lax.cond(
        (part[0] >= 0) & (part[0] < len(ROUTING_PLANES)),
        route,
        plain,
        *(part, even, own, weights, table, obs_cell, obs_count, obs_frac, obs_innov, obs_prec),
    )
    partials = lax.all_to_all(
        partials, "mem", split_axis=0, concat_axis=0, tiled=True, axis_index_groups=member_order
    )
    sources = [MEMBER_ORDER.index(plane) for plane in ROUTING_PLANES]
    (product,) = call(lambda *refs: obs_kernel(half, sources, *refs), [((flat, col_count), F32)], 0, 2)(partials, weights)
    near, far = neighbours(product)
    finish = call(lambda *refs: final_kernel(spread, rows, *refs), [((flat, col_count), F32)], 1, 5)
    (gradient,) = finish(even, own, product, near, far, table)
    return gradient.reshape(control.shape)


def solution(mesh):
    return jax.shard_map(
        per_device,
        mesh=mesh,
        in_specs=(
            P("mem", None, None, "tile"),
            P("mem", None, None, "tile"),
            P("tile", None, None),
            P("tile", None),
            P("tile", None, None, None),
            P("tile", None, None),
            P("tile", None, None),
        ),
        out_specs=P("mem", None, None, "tile"),
        check_vma=False,
    )
```

```python
import functools
import math

import jax
import jax.numpy as jnp
import ml_dtypes
import numpy as np
from jax import lax
from jax.experimental import pallas as pl
from jax.experimental.pallas import tpu as pltpu
from jax.sharding import PartitionSpec as P

YSCALE = 1
F32 = jnp.float32
BF16 = jnp.bfloat16
ROUTING_PLANES = (0, 1)
FIRST_BLOCKS = (5, 6, 7, 0, 1, 2, 3, 4)
SECOND_BLOCKS = (5, 6, 7, 0, 1, 2, 3, 4)
MEMBER_ORDER = (7, 6, 4, 5, 1, 0, 3, 2)


def halves(table):
    high = table.astype(np.float32).astype(ml_dtypes.bfloat16)
    low = (table.astype(np.float32) - high.astype(np.float32)).astype(ml_dtypes.bfloat16)
    return high, low


def tables(col_count, row_count, scale, levels):
    offset = (np.arange(3 * col_count) - col_count)[:, None] - np.arange(col_count)[None, :]
    band = np.where(np.abs(offset) <= col_count, np.exp(-0.5 * (offset / col_count) ** 2), 0.0)
    row_offset = np.arange(row_count)[:, None] - np.arange(row_count)[None, :]
    rows = np.exp(-0.5 * (row_offset / scale) ** 2)
    along_x = np.arange(-col_count, col_count + 1)
    along_y = np.arange(-(row_count - 1), row_count)
    total = np.sum(np.exp(-((along_x / col_count) ** 2))) * np.sum(np.exp(-((along_y / scale) ** 2)))
    mixed = np.kron(np.eye(levels), rows) / np.sqrt(total)
    mixed = np.tile(mixed, (1, col_count // mixed.shape[1]))
    return np.concatenate([*halves(band), *halves(mixed)], axis=0)


def split(values):
    high = values.astype(BF16)
    return high, (values - high.astype(F32)).astype(BF16)


def localize(high, low, table_ref, rows):
    flat, depth = high.shape
    cols = table_ref.shape[1]
    row_block = lax.broadcasted_iota(jnp.int32, (flat, flat), 0) // rows
    same = row_block == lax.broadcasted_iota(jnp.int32, (flat, flat), 1) // rows

    def mixing(start):
        strip = table_ref[start : start + rows].astype(F32)
        strip = jnp.concatenate([strip] * pl.cdiv(flat, cols), axis=1)[:, :flat]
        return jnp.where(same, jnp.concatenate([strip] * (flat // rows), axis=0), 0.0).astype(BF16)

    mixed_high, mixed_low = mixing(2 * depth), mixing(2 * depth + rows)
    band_high, band_low = table_ref[:depth], table_ref[depth : 2 * depth]
    swept = jnp.dot(
        jnp.concatenate([high, low, high], axis=1),
        jnp.concatenate([band_high, band_high, band_low], axis=0),
        preferred_element_type=F32,
    )
    high, low = split(swept)
    both = jnp.dot(mixed_high, jnp.concatenate([high, low], axis=1), preferred_element_type=F32)
    return both[:, :cols] + both[:, cols:] + jnp.dot(mixed_low, high, preferred_element_type=F32)


def extend(even, own, near, far):
    left = jnp.where(even, far, near)
    right = jnp.where(even, near, far)
    return jnp.concatenate([left, own, right], axis=1)


def payload_kernel(own_ref, perturb_ref, out_ref):
    flat = own_ref.shape[0]
    high, low = split(own_ref[...])
    out_ref[:flat] = high
    out_ref[flat : 2 * flat] = low
    out_ref[2 * flat :] = perturb_ref[...]


def pack_kernel(
    blocks, part, own_ref, perturb_ref, cell_ref, count_ref, frac_ref, innov_ref, prec_ref, payload_ref, out_ref
):
    payload_kernel(own_ref, perturb_ref, payload_ref)
    tiles = innov_ref.shape[1]
    slots = innov_ref.shape[0] // len(ROUTING_PLANES)
    cols = out_ref.shape[1]
    mine = slice(part * slots, (part + 1) * slots)
    slot = part * slots + lax.broadcasted_iota(jnp.int32, (slots, tiles), 0)
    live = jnp.where(slot < count_ref[...], 1.0, 0.0)
    cell = cell_ref[mine]
    corner_row = lax.shift_right_logical(cell, int(math.log2(cols)))
    corner_col = lax.bitwise_and(cell, cols - 1)
    packed = jnp.concatenate(
        [
            corner_col.astype(F32) + frac_ref[0, mine],
            corner_row.astype(F32) + frac_ref[1, mine],
            innov_ref[mine],
            prec_ref[mine] * live,
            jnp.zeros((out_ref.shape[1] - 4 * slots, tiles), F32),
        ],
        axis=0,
    )
    turned = jnp.transpose(packed)
    size = tiles // len(blocks)
    for place, block in enumerate(blocks):
        out_ref[place * size : (place + 1) * size] = turned[block * size : (block + 1) * size]


def partial_sum(spread, rows, even, own_ref, near_ref, far_ref, table_ref, kept_ref):
    flat = own_ref.shape[0] // 3
    high, low, perturb = (
        extend(even, *(ref[index * flat : (index + 1) * flat] for ref in (own_ref, near_ref, far_ref)))
        for index in range(3)
    )
    kept_ref[...] = perturb
    product = own_ref[2 * flat :].astype(F32) * localize(high, low, table_ref, rows)
    total = product[:rows]
    for start in range(rows, flat, rows):
        total = total + product[start : start + rows]
    return spread * total


def partial_kernel(spread, even_ref, own_ref, near_ref, far_ref, table_ref, out_ref, kept_ref):
    even = even_ref[0] == 1
    out_ref[...] = partial_sum(spread, out_ref.shape[0], even, own_ref, near_ref, far_ref, table_ref, kept_ref)


def partial_copies_kernel(spread, rows, even_ref, own_ref, near_ref, far_ref, table_ref, out_ref, kept_ref):
    even = even_ref[0] == 1
    total = partial_sum(spread, rows, even, own_ref, near_ref, far_ref, table_ref, kept_ref)
    for copy in range(out_ref.shape[0]):
        out_ref[copy, :rows] = total
        out_ref[copy, rows:] = jnp.zeros((out_ref.shape[1] - rows, out_ref.shape[2]), F32)


def join_kernel(partial_ref, obs_ref, out_ref):
    rows = partial_ref.shape[0]
    slots = (out_ref.shape[1] - rows) // 2
    total = partial_ref[...]
    turned = jnp.transpose(obs_ref[...])
    places = jnp.concatenate([turned[:slots], turned[slots : 2 * slots]], axis=1)
    values = jnp.concatenate([turned[2 * slots : 3 * slots], turned[3 * slots : 4 * slots]], axis=1)
    for copy in range(out_ref.shape[0]):
        out_ref[copy, :rows] = total
        out_ref[copy, rows : rows + slots] = places
        out_ref[copy, rows + slots :] = values


def obs_kernel(half, sources, partial_ref, out_ref):
    rows = partial_ref.shape[1] - 2 * half
    field = partial_ref[0, :rows]
    for member in range(1, partial_ref.shape[0]):
        field = field + partial_ref[member, :rows]
    cols = field.shape[1]
    tiles = cols // 2

    def quantity(start, lane):
        parts = [partial_ref[source, rows + start : rows + start + half] for source in sources]
        return jnp.concatenate([part[:, lane : lane + tiles] for part in parts], axis=1)

    at_x, at_y, innov, prec = quantity(0, 0), quantity(0, tiles), quantity(half, 0), quantity(half, tiles)
    corner_col, corner_row = at_x.astype(jnp.int32), at_y.astype(jnp.int32)
    frac_x, frac_y = at_x - corner_col.astype(F32), at_y - corner_row.astype(F32)
    lanes = at_x.shape[1]
    row_at = lax.broadcasted_iota(jnp.int32, (rows, lanes), 0)
    col_at = lax.broadcasted_iota(jnp.int32, (cols, lanes), 0)
    row_parts, col_parts = [], []
    for k in range(half):
        r, x = corner_row[k : k + 1], corner_col[k : k + 1]
        fy, fx = frac_y[k : k + 1], frac_x[k : k + 1]
        row_parts.append(jnp.where(row_at == r, 1.0 - fy, jnp.where(row_at == r + 1, fy, 0.0)))
        col_parts.append(jnp.where(col_at == x, 1.0 - fx, jnp.where(col_at == x + 1, fx, 0.0)))
    row_all = jnp.concatenate(row_parts, axis=1)
    row_high, row_low = split(row_all)
    field_high, field_low = split(jnp.transpose(field))
    picked = jnp.dot(
        jnp.concatenate([field_high, field_low, field_high], axis=1),
        jnp.concatenate([row_high, row_high, row_low], axis=0),
        preferred_element_type=F32,
    )
    weighted = []
    for k in range(half):
        value = jnp.sum(picked[:, k * lanes : (k + 1) * lanes] * col_parts[k], axis=0, keepdims=True)
        weighted.append(prec[k : k + 1] * (value - innov[k : k + 1]))
    weighted = jnp.concatenate(weighted, axis=1)
    rows_high, rows_low = split(row_all * weighted)
    cols_high, cols_low = split(jnp.concatenate(col_parts, axis=1))
    contract = (((1,), (1,)), ((), ()))
    both = jnp.concatenate([rows_high, rows_low], axis=0)
    both = lax.dot_general(both, cols_high, contract, preferred_element_type=F32)
    rest = lax.dot_general(rows_high, cols_low, contract, preferred_element_type=F32)
    out_ref[...] = both[:rows] + both[rows:] + rest


def final_kernel(spread, even_ref, control_ref, own_ref, near_ref, far_ref, kept_ref, table_ref, out_ref):
    even = even_ref[0] == 1
    rows = own_ref.shape[0]
    adjoint = extend(even, own_ref[...], near_ref[...], far_ref[...])
    adjoint = jnp.concatenate([adjoint] * (out_ref.shape[0] // rows), axis=0)
    high, low = split(kept_ref[...].astype(F32) * adjoint)
    out_ref[...] = control_ref[...] + spread * localize(high, low, table_ref, rows)


def call(kernel, out_shapes, scalars, arrays, flops=None):
    specs = [pl.BlockSpec(memory_space=pltpu.SMEM)] * scalars + [pl.BlockSpec(memory_space=pltpu.VMEM)] * arrays
    outs = [jax.ShapeDtypeStruct(shape, dtype) for shape, dtype in out_shapes]
    return pl.pallas_call(
        kernel,
        out_shape=outs,
        in_specs=specs,
        out_specs=[pl.BlockSpec(memory_space=pltpu.VMEM)] * len(outs),
        compiler_params=pltpu.CompilerParams(vmem_limit_bytes=24 * 1024 * 1024),
        cost_estimate=flops and pl.CostEstimate(flops=flops, bytes_accessed=0, transcendentals=0),
    )


def in_hbm(array):
    return pltpu.with_memory_space_constraint(array, pltpu.HBM)


def per_device(perturb, control, obs_cell, obs_count, obs_frac, obs_innov, obs_prec):
    mem_local, levels, row_count, col_count = perturb.shape
    members = lax.axis_size("mem")
    tiles = lax.axis_size("tile")
    spread = 1.0 / math.sqrt(mem_local * members - 1)
    slots = obs_cell.shape[2]
    rows = levels * row_count
    table = jnp.asarray(tables(col_count, row_count, YSCALE, levels))
    even = (1 - lax.axis_index("tile") % 2).astype(jnp.int32).reshape(1)
    member_order = [list(MEMBER_ORDER)]
    near_pairs = [(i, i ^ 1) for i in range(tiles)]
    far_pairs = [(i, (i + 1) % tiles if i % 2 else (i - 1) % tiles) for i in range(tiles)]

    def neighbours(own):
        far = lax.ppermute(own, "tile", far_pairs)
        return lax.ppermute(own, "tile", near_pairs), far

    flat = mem_local * rows
    half = slots // len(ROUTING_PLANES)
    joined = (members, rows + 2 * half, col_count)

    kept = ((flat, 3 * col_count), BF16)
    payload = ((3 * flat, col_count), BF16)

    def route(part, blocks, even, own, weights, table, cell, count, frac, innov, prec):
        size = tiles // len(blocks)
        tile_order = [[block * size + i for block in blocks for i in range(size)]]
        obs = (cell[0].T, count, frac[0].transpose(0, 2, 1), innov[0].T, prec[0].T)
        packed = ((tiles, col_count), F32)
        pack = call(lambda *refs: pack_kernel(blocks, part, *refs), [payload, packed], 0, 7, 10**9)
        sent, packed = pack(*map(in_hbm, (own, weights, *obs)))
        near, far = neighbours(sent)
        packed = packed.reshape(tiles, 1, col_count)
        arrived = lax.all_to_all(
            packed, "tile", split_axis=0, concat_axis=0, tiled=True, axis_index_groups=tile_order
        )
        summing = call(lambda *refs: partial_kernel(spread, *refs), [((rows, col_count), F32), kept], 1, 4, 1000)
        partial, weights = summing(even, sent, near, far, table)
        (partials,) = call(join_kernel, [(joined, F32)], 0, 2)(partial, arrived.reshape(tiles, col_count))
        return partials, weights

    def plain(even, own, weights, table, cell, count, frac, innov, prec):
        (sent,) = call(payload_kernel, [payload], 0, 2, 10**9)(in_hbm(own), in_hbm(weights))
        near, far = neighbours(sent)
        summing = call(lambda *refs: partial_copies_kernel(spread, rows, *refs), [(joined, F32), kept], 1, 4)
        return tuple(summing(even, sent, near, far, table))

    own = control.reshape(flat, col_count)
    weights = perturb.reshape(flat, col_count)
    plane = lax.axis_index("mem")
    branches = [functools.partial(route, part, blocks) for part, blocks in enumerate((FIRST_BLOCKS, SECOND_BLOCKS))]
    which = jnp.where(plane == ROUTING_PLANES[0], 0, jnp.where(plane == ROUTING_PLANES[1], 1, 2))
    partials, weights = lax.switch(
        which, [*branches, plain], even, own, weights, table, obs_cell, obs_count, obs_frac, obs_innov, obs_prec
    )
    partials = lax.all_to_all(
        partials, "mem", split_axis=0, concat_axis=0, tiled=True, axis_index_groups=member_order
    )
    sources = [MEMBER_ORDER.index(plane) for plane in ROUTING_PLANES]
    (adjoint,) = call(lambda *refs: obs_kernel(half, sources, *refs), [((rows, col_count), F32)], 0, 1)(partials)
    near, far = neighbours(adjoint)
    finish = call(lambda *refs: final_kernel(spread, *refs), [((flat, col_count), F32)], 1, 6)
    (gradient,) = finish(even, own, adjoint, near, far, weights, table)
    return gradient.reshape(control.shape)


def solution(mesh):
    return jax.shard_map(
        per_device,
        mesh=mesh,
        in_specs=(
            P("mem", None, None, "tile"),
            P("mem", None, None, "tile"),
            P("tile", None, None),
            P("tile", None),
            P("tile", None, None, None),
            P("tile", None, None),
            P("tile", None, None),
        ),
        out_specs=P("mem", None, None, "tile"),
        check_vma=False,
    )
```

```python
import functools
import math

import jax
import jax.numpy as jnp
import ml_dtypes
import numpy as np
from jax import lax
from jax.experimental import pallas as pl
from jax.experimental.pallas import tpu as pltpu
from jax.sharding import PartitionSpec as P

YSCALE = 1
F32 = jnp.float32
BF16 = jnp.bfloat16
ROUTING_PLANES = (0, 1)
FIRST_BLOCKS = (5, 6, 7, 0, 1, 2, 3, 4)
SECOND_BLOCKS = (5, 6, 7, 0, 1, 2, 3, 4)
WIDE = 3
FAR_PAD = 400
MEMBER_ORDER = (7, 6, 4, 5, 1, 0, 3, 2)


def halves(table):
    high = table.astype(np.float32).astype(ml_dtypes.bfloat16)
    low = (table.astype(np.float32) - high.astype(np.float32)).astype(ml_dtypes.bfloat16)
    return high, low


def tables(col_count, row_count, scale, levels):
    offset = (np.arange(3 * col_count) - col_count)[:, None] - np.arange(col_count)[None, :]
    band = np.where(np.abs(offset) <= col_count, np.exp(-0.5 * (offset / col_count) ** 2), 0.0)
    row_offset = np.arange(row_count)[:, None] - np.arange(row_count)[None, :]
    rows = np.exp(-0.5 * (row_offset / scale) ** 2)
    along_x = np.arange(-col_count, col_count + 1)
    along_y = np.arange(-(row_count - 1), row_count)
    total = np.sum(np.exp(-((along_x / col_count) ** 2))) * np.sum(np.exp(-((along_y / scale) ** 2)))
    mixed = np.kron(np.eye(levels), rows) / np.sqrt(total)
    mixed = np.tile(mixed, (1, col_count // mixed.shape[1]))
    return np.concatenate([*halves(band), *halves(mixed)], axis=0)


def split(values):
    high = values.astype(BF16)
    return high, (values - high.astype(F32)).astype(BF16)


def localize(high, low, table_ref, rows):
    flat, depth = high.shape
    cols = table_ref.shape[1]
    row_block = lax.broadcasted_iota(jnp.int32, (flat, flat), 0) // rows
    same = row_block == lax.broadcasted_iota(jnp.int32, (flat, flat), 1) // rows

    def mixing(start):
        strip = table_ref[start : start + rows].astype(F32)
        strip = jnp.concatenate([strip] * pl.cdiv(flat, cols), axis=1)[:, :flat]
        return jnp.where(same, jnp.concatenate([strip] * (flat // rows), axis=0), 0.0).astype(BF16)

    mixed_high, mixed_low = mixing(2 * depth), mixing(2 * depth + rows)
    band_high, band_low = table_ref[:depth], table_ref[depth : 2 * depth]
    swept = jnp.dot(
        jnp.concatenate([high, low, high], axis=1),
        jnp.concatenate([band_high, band_high, band_low], axis=0),
        preferred_element_type=F32,
    )
    high, low = split(swept)
    both = jnp.dot(mixed_high, jnp.concatenate([high, low], axis=1), preferred_element_type=F32)
    return both[:, :cols] + both[:, cols:] + jnp.dot(mixed_low, high, preferred_element_type=F32)


def extend(even, own, near, far):
    left = jnp.where(even, far, near)
    right = jnp.where(even, near, far)
    return jnp.concatenate([left, own, right], axis=1)


def payload_kernel(own_ref, perturb_ref, out_ref):
    flat = own_ref.shape[0]
    high, low = split(own_ref[...])
    out_ref[:flat] = high
    out_ref[flat : 2 * flat] = low
    out_ref[2 * flat :] = perturb_ref[...]


def pack_kernel(
    blocks, part, own_ref, perturb_ref, cell_ref, count_ref, frac_ref, innov_ref, prec_ref, payload_ref, wider_ref, out_ref
):
    payload_kernel(own_ref, perturb_ref, payload_ref)
    length = payload_ref.shape[0]
    wider_ref[:length] = payload_ref[...]
    wider_ref[length:] = jnp.zeros((wider_ref.shape[0] - length, wider_ref.shape[1]), BF16)
    tiles = innov_ref.shape[1]
    slots = innov_ref.shape[0] // len(ROUTING_PLANES)
    cols = payload_ref.shape[1]
    mine = slice(part * slots, (part + 1) * slots)
    slot = part * slots + lax.broadcasted_iota(jnp.int32, (slots, tiles), 0)
    live = jnp.where(slot < count_ref[...], 1.0, 0.0)
    cell = cell_ref[mine]
    corner_row = lax.shift_right_logical(cell, int(math.log2(cols)))
    corner_col = lax.bitwise_and(cell, cols - 1)
    packed = jnp.concatenate(
        [
            corner_col.astype(F32) + frac_ref[0, mine],
            corner_row.astype(F32) + frac_ref[1, mine],
            innov_ref[mine],
            prec_ref[mine] * live,
            jnp.zeros((cols - 4 * slots, tiles), F32),
        ],
        axis=0,
    )
    turned = jnp.transpose(packed)
    size = tiles // len(blocks)
    for place, block in enumerate(blocks):
        out_ref[place * size : (place + 1) * size, 0, :cols] = turned[block * size : (block + 1) * size]
    out_ref[:, 0, cols:] = jnp.zeros((tiles, out_ref.shape[2] - cols), F32)


def partial_sum(spread, rows, even, own_ref, near_ref, far_ref, table_ref, kept_ref):
    flat = own_ref.shape[0] // 3
    high, low, perturb = (
        extend(even, *(ref[index * flat : (index + 1) * flat] for ref in (own_ref, near_ref, far_ref)))
        for index in range(3)
    )
    kept_ref[...] = perturb
    product = own_ref[2 * flat :].astype(F32) * localize(high, low, table_ref, rows)
    total = product[:rows]
    for start in range(rows, flat, rows):
        total = total + product[start : start + rows]
    return spread * total


def partial_kernel(spread, even_ref, own_ref, near_ref, far_ref, table_ref, out_ref, kept_ref):
    even = even_ref[0] == 1
    out_ref[...] = partial_sum(spread, out_ref.shape[0], even, own_ref, near_ref, far_ref, table_ref, kept_ref)


def partial_copies_kernel(spread, rows, even_ref, own_ref, near_ref, far_ref, table_ref, out_ref, kept_ref):
    even = even_ref[0] == 1
    total = partial_sum(spread, rows, even, own_ref, near_ref, far_ref, table_ref, kept_ref)
    for copy in range(out_ref.shape[0]):
        out_ref[copy, :rows] = total
        out_ref[copy, rows:] = jnp.zeros((out_ref.shape[1] - rows, out_ref.shape[2]), F32)


def join_kernel(partial_ref, obs_ref, out_ref):
    rows = partial_ref.shape[0]
    slots = (out_ref.shape[1] - rows) // 2
    total = partial_ref[...]
    turned = jnp.transpose(obs_ref[:, 0, : partial_ref.shape[1]])
    places = jnp.concatenate([turned[:slots], turned[slots : 2 * slots]], axis=1)
    values = jnp.concatenate([turned[2 * slots : 3 * slots], turned[3 * slots : 4 * slots]], axis=1)
    for copy in range(out_ref.shape[0]):
        out_ref[copy, :rows] = total
        out_ref[copy, rows : rows + slots] = places
        out_ref[copy, rows + slots :] = values


def obs_kernel(half, sources, partial_ref, out_ref):
    rows = partial_ref.shape[1] - 2 * half
    field = partial_ref[0, :rows]
    for member in range(1, partial_ref.shape[0]):
        field = field + partial_ref[member, :rows]
    cols = field.shape[1]
    tiles = cols // 2

    def quantity(start, lane):
        parts = [partial_ref[source, rows + start : rows + start + half] for source in sources]
        return jnp.concatenate([part[:, lane : lane + tiles] for part in parts], axis=1)

    at_x, at_y, innov, prec = quantity(0, 0), quantity(0, tiles), quantity(half, 0), quantity(half, tiles)
    corner_col, corner_row = at_x.astype(jnp.int32), at_y.astype(jnp.int32)
    frac_x, frac_y = at_x - corner_col.astype(F32), at_y - corner_row.astype(F32)
    lanes = at_x.shape[1]
    row_at = lax.broadcasted_iota(jnp.int32, (rows, lanes), 0)
    col_at = lax.broadcasted_iota(jnp.int32, (cols, lanes), 0)
    row_parts, col_parts = [], []
    for k in range(half):
        r, x = corner_row[k : k + 1], corner_col[k : k + 1]
        fy, fx = frac_y[k : k + 1], frac_x[k : k + 1]
        row_parts.append(jnp.where(row_at == r, 1.0 - fy, jnp.where(row_at == r + 1, fy, 0.0)))
        col_parts.append(jnp.where(col_at == x, 1.0 - fx, jnp.where(col_at == x + 1, fx, 0.0)))
    row_all = jnp.concatenate(row_parts, axis=1)
    row_high, row_low = split(row_all)
    field_high, field_low = split(jnp.transpose(field))
    picked = jnp.dot(
        jnp.concatenate([field_high, field_low, field_high], axis=1),
        jnp.concatenate([row_high, row_high, row_low], axis=0),
        preferred_element_type=F32,
    )
    weighted = []
    for k in range(half):
        value = jnp.sum(picked[:, k * lanes : (k + 1) * lanes] * col_parts[k], axis=0, keepdims=True)
        weighted.append(prec[k : k + 1] * (value - innov[k : k + 1]))
    weighted = jnp.concatenate(weighted, axis=1)
    rows_high, rows_low = split(row_all * weighted)
    cols_high, cols_low = split(jnp.concatenate(col_parts, axis=1))
    contract = (((1,), (1,)), ((), ()))
    both = jnp.concatenate([rows_high, rows_low], axis=0)
    both = lax.dot_general(both, cols_high, contract, preferred_element_type=F32)
    rest = lax.dot_general(rows_high, cols_low, contract, preferred_element_type=F32)
    out_ref[...] = both[:rows] + both[rows:] + rest


def final_kernel(spread, even_ref, control_ref, own_ref, near_ref, far_ref, kept_ref, table_ref, out_ref):
    even = even_ref[0] == 1
    rows = own_ref.shape[0]
    adjoint = extend(even, own_ref[...], near_ref[...], far_ref[...])
    adjoint = jnp.concatenate([adjoint] * (out_ref.shape[0] // rows), axis=0)
    high, low = split(kept_ref[...].astype(F32) * adjoint)
    out_ref[...] = control_ref[...] + spread * localize(high, low, table_ref, rows)


def call(kernel, out_shapes, scalars, arrays, flops=None):
    specs = [pl.BlockSpec(memory_space=pltpu.SMEM)] * scalars + [pl.BlockSpec(memory_space=pltpu.VMEM)] * arrays
    outs = [jax.ShapeDtypeStruct(shape, dtype) for shape, dtype in out_shapes]
    return pl.pallas_call(
        kernel,
        out_shape=outs,
        in_specs=specs,
        out_specs=[pl.BlockSpec(memory_space=pltpu.VMEM)] * len(outs),
        compiler_params=pltpu.CompilerParams(vmem_limit_bytes=24 * 1024 * 1024),
        cost_estimate=flops and pl.CostEstimate(flops=flops, bytes_accessed=0, transcendentals=0),
    )


def in_hbm(array):
    return pltpu.with_memory_space_constraint(array, pltpu.HBM)


def per_device(perturb, control, obs_cell, obs_count, obs_frac, obs_innov, obs_prec):
    mem_local, levels, row_count, col_count = perturb.shape
    members = lax.axis_size("mem")
    tiles = lax.axis_size("tile")
    spread = 1.0 / math.sqrt(mem_local * members - 1)
    slots = obs_cell.shape[2]
    rows = levels * row_count
    table = jnp.asarray(tables(col_count, row_count, YSCALE, levels))
    even = (1 - lax.axis_index("tile") % 2).astype(jnp.int32).reshape(1)
    member_order = [list(MEMBER_ORDER)]
    near_pairs = [(i, i ^ 1) for i in range(tiles)]
    far_pairs = [(i, (i + 1) % tiles if i % 2 else (i - 1) % tiles) for i in range(tiles)]

    def neighbours(own):
        far = lax.ppermute(own, "tile", far_pairs)
        return lax.ppermute(own, "tile", near_pairs), far

    flat = mem_local * rows
    half = slots // len(ROUTING_PLANES)
    joined = (members, rows + 2 * half, col_count)

    kept = ((flat, 3 * col_count), BF16)
    payload = ((3 * flat, col_count), BF16)

    def route(part, blocks, even, own, weights, table, cell, count, frac, innov, prec):
        size = tiles // len(blocks)
        tile_order = [[block * size + i for block in blocks for i in range(size)]]
        obs = (cell[0].T, count, frac[0].transpose(0, 2, 1), innov[0].T, prec[0].T)
        packed = ((tiles, 1, WIDE * col_count), F32)
        wider = ((3 * flat + FAR_PAD, col_count), BF16)
        pack = call(lambda *refs: pack_kernel(blocks, part, *refs), [payload, wider, packed], 0, 7, 10**9)
        sent, sent_far, packed = pack(*map(in_hbm, (own, weights, *obs)))
        far = lax.ppermute(sent_far, "tile", far_pairs)
        near = lax.ppermute(sent, "tile", near_pairs)
        arrived = lax.all_to_all(
            packed, "tile", split_axis=0, concat_axis=0, tiled=True, axis_index_groups=tile_order
        )
        summing = call(lambda *refs: partial_kernel(spread, *refs), [((rows, col_count), F32), kept], 1, 4, 1000)
        partial, weights = summing(even, sent, near, far, table)
        (partials,) = call(join_kernel, [(joined, F32)], 0, 2)(partial, arrived)
        return partials, weights

    def plain(even, own, weights, table, cell, count, frac, innov, prec):
        (sent,) = call(payload_kernel, [payload], 0, 2, 10**9)(in_hbm(own), in_hbm(weights))
        near, far = neighbours(sent)
        summing = call(lambda *refs: partial_copies_kernel(spread, rows, *refs), [(joined, F32), kept], 1, 4)
        return tuple(summing(even, sent, near, far, table))

    own = control.reshape(flat, col_count)
    weights = perturb.reshape(flat, col_count)
    plane = lax.axis_index("mem")
    branches = [functools.partial(route, part, blocks) for part, blocks in enumerate((FIRST_BLOCKS, SECOND_BLOCKS))]
    which = jnp.where(plane == ROUTING_PLANES[0], 0, jnp.where(plane == ROUTING_PLANES[1], 1, 2))
    partials, weights = lax.switch(
        which, [*branches, plain], even, own, weights, table, obs_cell, obs_count, obs_frac, obs_innov, obs_prec
    )
    partials = lax.all_to_all(
        partials, "mem", split_axis=0, concat_axis=0, tiled=True, axis_index_groups=member_order
    )
    sources = [MEMBER_ORDER.index(plane) for plane in ROUTING_PLANES]
    (adjoint,) = call(lambda *refs: obs_kernel(half, sources, *refs), [((rows, col_count), F32)], 0, 1)(partials)
    near, far = neighbours(adjoint)
    finish = call(lambda *refs: final_kernel(spread, *refs), [((flat, col_count), F32)], 1, 6)
    (gradient,) = finish(even, own, adjoint, near, far, weights, table)
    return gradient.reshape(control.shape)


def solution(mesh):
    return jax.shard_map(
        per_device,
        mesh=mesh,
        in_specs=(
            P("mem", None, None, "tile"),
            P("mem", None, None, "tile"),
            P("tile", None, None),
            P("tile", None),
            P("tile", None, None, None),
            P("tile", None, None),
            P("tile", None, None),
        ),
        out_specs=P("mem", None, None, "tile"),
        check_vma=False,
    )
```

```python
import functools
import math

import jax
import jax.numpy as jnp
import ml_dtypes
import numpy as np
from jax import lax
from jax.experimental import pallas as pl
from jax.experimental.pallas import tpu as pltpu
from jax.sharding import PartitionSpec as P

YSCALE = 1
F32 = jnp.float32
BF16 = jnp.bfloat16
ROUTING_PLANES = (0, 1)
FIRST_BLOCKS = (5, 0, 7, 6, 1, 2, 3, 4)
SECOND_BLOCKS = (5, 0, 7, 6, 1, 2, 3, 4)
WIDE = 3
FAR_PAD = 400
MEMBER_ORDER = (7, 6, 4, 5, 1, 0, 3, 2)


def halves(table):
    high = table.astype(np.float32).astype(ml_dtypes.bfloat16)
    low = (table.astype(np.float32) - high.astype(np.float32)).astype(ml_dtypes.bfloat16)
    return high, low


def tables(col_count, row_count, scale, levels):
    offset = (np.arange(3 * col_count) - col_count)[:, None] - np.arange(col_count)[None, :]
    band = np.where(np.abs(offset) <= col_count, np.exp(-0.5 * (offset / col_count) ** 2), 0.0)
    row_offset = np.arange(row_count)[:, None] - np.arange(row_count)[None, :]
    rows = np.exp(-0.5 * (row_offset / scale) ** 2)
    along_x = np.arange(-col_count, col_count + 1)
    along_y = np.arange(-(row_count - 1), row_count)
    total = np.sum(np.exp(-((along_x / col_count) ** 2))) * np.sum(np.exp(-((along_y / scale) ** 2)))
    mixed = np.kron(np.eye(levels), rows) / np.sqrt(total)
    mixed = np.tile(mixed, (1, col_count // mixed.shape[1]))
    return np.concatenate([*halves(band), *halves(mixed)], axis=0)


def split(values):
    high = values.astype(BF16)
    return high, (values - high.astype(F32)).astype(BF16)


def localize(high, low, table_ref, rows):
    flat, depth = high.shape
    cols = table_ref.shape[1]
    row_block = lax.broadcasted_iota(jnp.int32, (flat, flat), 0) // rows
    same = row_block == lax.broadcasted_iota(jnp.int32, (flat, flat), 1) // rows

    def mixing(start):
        strip = table_ref[start : start + rows].astype(F32)
        strip = jnp.concatenate([strip] * pl.cdiv(flat, cols), axis=1)[:, :flat]
        return jnp.where(same, jnp.concatenate([strip] * (flat // rows), axis=0), 0.0).astype(BF16)

    mixed_high, mixed_low = mixing(2 * depth), mixing(2 * depth + rows)
    band_high, band_low = table_ref[:depth], table_ref[depth : 2 * depth]
    swept = jnp.dot(
        jnp.concatenate([high, low, high], axis=1),
        jnp.concatenate([band_high, band_high, band_low], axis=0),
        preferred_element_type=F32,
    )
    high, low = split(swept)
    both = jnp.dot(mixed_high, jnp.concatenate([high, low], axis=1), preferred_element_type=F32)
    return both[:, :cols] + both[:, cols:] + jnp.dot(mixed_low, high, preferred_element_type=F32)


def extend(even, own, near, far):
    left = jnp.where(even, far, near)
    right = jnp.where(even, near, far)
    return jnp.concatenate([left, own, right], axis=1)


def payload_kernel(own_ref, perturb_ref, out_ref):
    flat = own_ref.shape[0]
    high, low = split(own_ref[...])
    out_ref[:flat] = high
    out_ref[flat : 2 * flat] = low
    out_ref[2 * flat :] = perturb_ref[...]


def pack_kernel(
    blocks, part, own_ref, perturb_ref, cell_ref, count_ref, frac_ref, innov_ref, prec_ref, payload_ref, wider_ref, out_ref
):
    payload_kernel(own_ref, perturb_ref, payload_ref)
    length = payload_ref.shape[0]
    wider_ref[:length] = payload_ref[...]
    wider_ref[length:] = jnp.zeros((wider_ref.shape[0] - length, wider_ref.shape[1]), BF16)
    tiles = innov_ref.shape[1]
    slots = innov_ref.shape[0] // len(ROUTING_PLANES)
    cols = payload_ref.shape[1]
    mine = slice(part * slots, (part + 1) * slots)
    slot = part * slots + lax.broadcasted_iota(jnp.int32, (slots, tiles), 0)
    live = jnp.where(slot < count_ref[...], 1.0, 0.0)
    cell = cell_ref[mine]
    corner_row = lax.shift_right_logical(cell, int(math.log2(cols)))
    corner_col = lax.bitwise_and(cell, cols - 1)
    packed = jnp.concatenate(
        [
            corner_col.astype(F32) + frac_ref[0, mine],
            corner_row.astype(F32) + frac_ref[1, mine],
            innov_ref[mine],
            prec_ref[mine] * live,
            jnp.zeros((cols - 4 * slots, tiles), F32),
        ],
        axis=0,
    )
    turned = jnp.transpose(packed)
    size = tiles // len(blocks)
    for place, block in enumerate(blocks):
        out_ref[place * size : (place + 1) * size, 0, :cols] = turned[block * size : (block + 1) * size]
    out_ref[:, 0, cols:] = jnp.zeros((tiles, out_ref.shape[2] - cols), F32)


def partial_sum(spread, rows, even, own_ref, near_ref, far_ref, table_ref, kept_ref):
    flat = own_ref.shape[0] // 3
    high, low, perturb = (
        extend(even, *(ref[index * flat : (index + 1) * flat] for ref in (own_ref, near_ref, far_ref)))
        for index in range(3)
    )
    kept_ref[...] = perturb
    product = own_ref[2 * flat :].astype(F32) * localize(high, low, table_ref, rows)
    total = product[:rows]
    for start in range(rows, flat, rows):
        total = total + product[start : start + rows]
    return spread * total


def partial_kernel(spread, even_ref, own_ref, near_ref, far_ref, table_ref, out_ref, kept_ref):
    even = even_ref[0] == 1
    out_ref[...] = partial_sum(spread, out_ref.shape[0], even, own_ref, near_ref, far_ref, table_ref, kept_ref)


def partial_copies_kernel(spread, rows, even_ref, own_ref, near_ref, far_ref, table_ref, out_ref, kept_ref):
    even = even_ref[0] == 1
    total = partial_sum(spread, rows, even, own_ref, near_ref, far_ref, table_ref, kept_ref)
    for copy in range(out_ref.shape[0]):
        out_ref[copy, :rows] = total
        out_ref[copy, rows:] = jnp.zeros((out_ref.shape[1] - rows, out_ref.shape[2]), F32)


def join_kernel(partial_ref, obs_ref, out_ref):
    rows = partial_ref.shape[0]
    slots = (out_ref.shape[1] - rows) // 2
    total = partial_ref[...]
    turned = jnp.transpose(obs_ref[:, 0, : partial_ref.shape[1]])
    places = jnp.concatenate([turned[:slots], turned[slots : 2 * slots]], axis=1)
    values = jnp.concatenate([turned[2 * slots : 3 * slots], turned[3 * slots : 4 * slots]], axis=1)
    for copy in range(out_ref.shape[0]):
        out_ref[copy, :rows] = total
        out_ref[copy, rows : rows + slots] = places
        out_ref[copy, rows + slots :] = values


def obs_kernel(half, sources, partial_ref, out_ref):
    rows = partial_ref.shape[1] - 2 * half
    field = partial_ref[0, :rows]
    for member in range(1, partial_ref.shape[0]):
        field = field + partial_ref[member, :rows]
    cols = field.shape[1]
    tiles = cols // 2

    def quantity(start, lane):
        parts = [partial_ref[source, rows + start : rows + start + half] for source in sources]
        return jnp.concatenate([part[:, lane : lane + tiles] for part in parts], axis=1)

    at_x, at_y, innov, prec = quantity(0, 0), quantity(0, tiles), quantity(half, 0), quantity(half, tiles)
    corner_col, corner_row = at_x.astype(jnp.int32), at_y.astype(jnp.int32)
    frac_x, frac_y = at_x - corner_col.astype(F32), at_y - corner_row.astype(F32)
    lanes = at_x.shape[1]
    row_at = lax.broadcasted_iota(jnp.int32, (rows, lanes), 0)
    col_at = lax.broadcasted_iota(jnp.int32, (cols, lanes), 0)
    row_parts, col_parts = [], []
    for k in range(half):
        r, x = corner_row[k : k + 1], corner_col[k : k + 1]
        fy, fx = frac_y[k : k + 1], frac_x[k : k + 1]
        row_parts.append(jnp.where(row_at == r, 1.0 - fy, jnp.where(row_at == r + 1, fy, 0.0)))
        col_parts.append(jnp.where(col_at == x, 1.0 - fx, jnp.where(col_at == x + 1, fx, 0.0)))
    row_all = jnp.concatenate(row_parts, axis=1)
    row_high, row_low = split(row_all)
    field_high, field_low = split(jnp.transpose(field))
    picked = jnp.dot(
        jnp.concatenate([field_high, field_low, field_high], axis=1),
        jnp.concatenate([row_high, row_high, row_low], axis=0),
        preferred_element_type=F32,
    )
    weighted = []
    for k in range(half):
        value = jnp.sum(picked[:, k * lanes : (k + 1) * lanes] * col_parts[k], axis=0, keepdims=True)
        weighted.append(prec[k : k + 1] * (value - innov[k : k + 1]))
    weighted = jnp.concatenate(weighted, axis=1)
    rows_high, rows_low = split(row_all * weighted)
    cols_high, cols_low = split(jnp.concatenate(col_parts, axis=1))
    contract = (((1,), (1,)), ((), ()))
    both = jnp.concatenate([rows_high, rows_low], axis=0)
    both = lax.dot_general(both, cols_high, contract, preferred_element_type=F32)
    rest = lax.dot_general(rows_high, cols_low, contract, preferred_element_type=F32)
    out_ref[...] = both[:rows] + both[rows:] + rest


def final_kernel(spread, even_ref, control_ref, own_ref, near_ref, far_ref, kept_ref, table_ref, out_ref):
    even = even_ref[0] == 1
    rows = own_ref.shape[0]
    adjoint = extend(even, own_ref[...], near_ref[...], far_ref[...])
    adjoint = jnp.concatenate([adjoint] * (out_ref.shape[0] // rows), axis=0)
    high, low = split(kept_ref[...].astype(F32) * adjoint)
    out_ref[...] = control_ref[...] + spread * localize(high, low, table_ref, rows)


def call(kernel, out_shapes, scalars, arrays, flops=None):
    specs = [pl.BlockSpec(memory_space=pltpu.SMEM)] * scalars + [pl.BlockSpec(memory_space=pltpu.VMEM)] * arrays
    outs = [jax.ShapeDtypeStruct(shape, dtype) for shape, dtype in out_shapes]
    return pl.pallas_call(
        kernel,
        out_shape=outs,
        in_specs=specs,
        out_specs=[pl.BlockSpec(memory_space=pltpu.VMEM)] * len(outs),
        compiler_params=pltpu.CompilerParams(vmem_limit_bytes=24 * 1024 * 1024),
        cost_estimate=flops and pl.CostEstimate(flops=flops, bytes_accessed=0, transcendentals=0),
    )


def in_hbm(array):
    return pltpu.with_memory_space_constraint(array, pltpu.HBM)


def per_device(perturb, control, obs_cell, obs_count, obs_frac, obs_innov, obs_prec):
    mem_local, levels, row_count, col_count = perturb.shape
    members = lax.axis_size("mem")
    tiles = lax.axis_size("tile")
    spread = 1.0 / math.sqrt(mem_local * members - 1)
    slots = obs_cell.shape[2]
    rows = levels * row_count
    table = jnp.asarray(tables(col_count, row_count, YSCALE, levels))
    even = (1 - lax.axis_index("tile") % 2).astype(jnp.int32).reshape(1)
    member_order = [list(MEMBER_ORDER)]
    near_pairs = [(i, i ^ 1) for i in range(tiles)]
    far_pairs = [(i, (i + 1) % tiles if i % 2 else (i - 1) % tiles) for i in range(tiles)]

    def neighbours(own):
        far = lax.ppermute(own, "tile", far_pairs)
        return lax.ppermute(own, "tile", near_pairs), far

    flat = mem_local * rows
    half = slots // len(ROUTING_PLANES)
    joined = (members, rows + 2 * half, col_count)

    kept = ((flat, 3 * col_count), BF16)
    payload = ((3 * flat, col_count), BF16)

    def route(part, blocks, even, own, weights, table, cell, count, frac, innov, prec):
        size = tiles // len(blocks)
        tile_order = [[block * size + i for block in blocks for i in range(size)]]
        obs = (cell[0].T, count, frac[0].transpose(0, 2, 1), innov[0].T, prec[0].T)
        packed = ((tiles, 1, WIDE * col_count), F32)
        wider = ((3 * flat + FAR_PAD, col_count), BF16)
        pack = call(lambda *refs: pack_kernel(blocks, part, *refs), [payload, wider, packed], 0, 7, 10**9)
        sent, sent_far, packed = pack(*map(in_hbm, (own, weights, *obs)))
        far = lax.ppermute(sent_far, "tile", far_pairs)
        near = lax.ppermute(sent, "tile", near_pairs)
        arrived = lax.all_to_all(
            packed, "tile", split_axis=0, concat_axis=0, tiled=True, axis_index_groups=tile_order
        )
        summing = call(lambda *refs: partial_kernel(spread, *refs), [((rows, col_count), F32), kept], 1, 4, 1000)
        partial, weights = summing(even, sent, near, far, table)
        (partials,) = call(join_kernel, [(joined, F32)], 0, 2)(partial, arrived)
        return partials, weights

    def plain(even, own, weights, table, cell, count, frac, innov, prec):
        (sent,) = call(payload_kernel, [payload], 0, 2, 10**9)(in_hbm(own), in_hbm(weights))
        near, far = neighbours(sent)
        summing = call(lambda *refs: partial_copies_kernel(spread, rows, *refs), [(joined, F32), kept], 1, 4)
        return tuple(summing(even, sent, near, far, table))

    own = control.reshape(flat, col_count)
    weights = perturb.reshape(flat, col_count)
    plane = lax.axis_index("mem")
    branches = [functools.partial(route, part, blocks) for part, blocks in enumerate((FIRST_BLOCKS, SECOND_BLOCKS))]
    which = jnp.where(plane == ROUTING_PLANES[0], 0, jnp.where(plane == ROUTING_PLANES[1], 1, 2))
    partials, weights = lax.switch(
        which, [*branches, plain], even, own, weights, table, obs_cell, obs_count, obs_frac, obs_innov, obs_prec
    )
    partials = lax.all_to_all(
        partials, "mem", split_axis=0, concat_axis=0, tiled=True, axis_index_groups=member_order
    )
    sources = [MEMBER_ORDER.index(plane) for plane in ROUTING_PLANES]
    (adjoint,) = call(lambda *refs: obs_kernel(half, sources, *refs), [((rows, col_count), F32)], 0, 1)(partials)
    near, far = neighbours(adjoint)
    finish = call(lambda *refs: final_kernel(spread, *refs), [((flat, col_count), F32)], 1, 6)
    (gradient,) = finish(even, own, adjoint, near, far, weights, table)
    return gradient.reshape(control.shape)


def solution(mesh):
    return jax.shard_map(
        per_device,
        mesh=mesh,
        in_specs=(
            P("mem", None, None, "tile"),
            P("mem", None, None, "tile"),
            P("tile", None, None),
            P("tile", None),
            P("tile", None, None, None),
            P("tile", None, None),
            P("tile", None, None),
        ),
        out_specs=P("mem", None, None, "tile"),
        check_vma=False,
    )
```

```python
import functools
import math

import jax
import jax.numpy as jnp
import ml_dtypes
import numpy as np
from jax import lax
from jax.experimental import pallas as pl
from jax.experimental.pallas import tpu as pltpu
from jax.sharding import PartitionSpec as P

YSCALE = 1
F32 = jnp.float32
BF16 = jnp.bfloat16
ROUTING_PLANES = (0, 1)
FIRST_BLOCKS = (5, 0, 7, 1, 2, 6, 3, 4)
SECOND_BLOCKS = (5, 0, 7, 1, 2, 6, 3, 4)
WIDE = 3
FAR_PAD = 400
MEMBER_ORDER = (7, 6, 4, 5, 1, 0, 3, 2)


def halves(table):
    high = table.astype(np.float32).astype(ml_dtypes.bfloat16)
    low = (table.astype(np.float32) - high.astype(np.float32)).astype(ml_dtypes.bfloat16)
    return high, low


def tables(col_count, row_count, scale, levels):
    offset = (np.arange(3 * col_count) - col_count)[:, None] - np.arange(col_count)[None, :]
    band = np.where(np.abs(offset) <= col_count, np.exp(-0.5 * (offset / col_count) ** 2), 0.0)
    row_offset = np.arange(row_count)[:, None] - np.arange(row_count)[None, :]
    rows = np.exp(-0.5 * (row_offset / scale) ** 2)
    along_x = np.arange(-col_count, col_count + 1)
    along_y = np.arange(-(row_count - 1), row_count)
    total = np.sum(np.exp(-((along_x / col_count) ** 2))) * np.sum(np.exp(-((along_y / scale) ** 2)))
    mixed = np.kron(np.eye(levels), rows) / np.sqrt(total)
    mixed = np.tile(mixed, (1, col_count // mixed.shape[1]))
    return np.concatenate([*halves(band), *halves(mixed)], axis=0)


def split(values):
    high = values.astype(BF16)
    return high, (values - high.astype(F32)).astype(BF16)


def localize(high, low, table_ref, rows):
    flat, depth = high.shape
    cols = table_ref.shape[1]
    row_block = lax.broadcasted_iota(jnp.int32, (flat, flat), 0) // rows
    same = row_block == lax.broadcasted_iota(jnp.int32, (flat, flat), 1) // rows

    def mixing(start):
        strip = table_ref[start : start + rows].astype(F32)
        strip = jnp.concatenate([strip] * pl.cdiv(flat, cols), axis=1)[:, :flat]
        return jnp.where(same, jnp.concatenate([strip] * (flat // rows), axis=0), 0.0).astype(BF16)

    mixed_high, mixed_low = mixing(2 * depth), mixing(2 * depth + rows)
    band_high, band_low = table_ref[:depth], table_ref[depth : 2 * depth]
    swept = jnp.dot(
        jnp.concatenate([high, low, high], axis=1),
        jnp.concatenate([band_high, band_high, band_low], axis=0),
        preferred_element_type=F32,
    )
    high, low = split(swept)
    both = jnp.dot(mixed_high, jnp.concatenate([high, low], axis=1), preferred_element_type=F32)
    return both[:, :cols] + both[:, cols:] + jnp.dot(mixed_low, high, preferred_element_type=F32)


def extend(even, own, near, far):
    left = jnp.where(even, far, near)
    right = jnp.where(even, near, far)
    return jnp.concatenate([left, own, right], axis=1)


def payload_kernel(own_ref, perturb_ref, out_ref):
    flat = own_ref.shape[0]
    high, low = split(own_ref[...])
    out_ref[:flat] = high
    out_ref[flat : 2 * flat] = low
    out_ref[2 * flat :] = perturb_ref[...]


def pack_kernel(
    blocks, part, own_ref, perturb_ref, cell_ref, count_ref, frac_ref, innov_ref, prec_ref, payload_ref, wider_ref, out_ref
):
    payload_kernel(own_ref, perturb_ref, payload_ref)
    length = payload_ref.shape[0]
    wider_ref[:length] = payload_ref[...]
    wider_ref[length:] = jnp.zeros((wider_ref.shape[0] - length, wider_ref.shape[1]), BF16)
    tiles = innov_ref.shape[1]
    slots = innov_ref.shape[0] // len(ROUTING_PLANES)
    cols = payload_ref.shape[1]
    mine = slice(part * slots, (part + 1) * slots)
    slot = part * slots + lax.broadcasted_iota(jnp.int32, (slots, tiles), 0)
    live = jnp.where(slot < count_ref[...], 1.0, 0.0)
    cell = cell_ref[mine]
    corner_row = lax.shift_right_logical(cell, int(math.log2(cols)))
    corner_col = lax.bitwise_and(cell, cols - 1)
    packed = jnp.concatenate(
        [
            corner_col.astype(F32) + frac_ref[0, mine],
            corner_row.astype(F32) + frac_ref[1, mine],
            innov_ref[mine],
            prec_ref[mine] * live,
            jnp.zeros((cols - 4 * slots, tiles), F32),
        ],
        axis=0,
    )
    turned = jnp.transpose(packed)
    size = tiles // len(blocks)
    for place, block in enumerate(blocks):
        out_ref[place * size : (place + 1) * size, 0, :cols] = turned[block * size : (block + 1) * size]
    out_ref[:, 0, cols:] = jnp.zeros((tiles, out_ref.shape[2] - cols), F32)


def partial_sum(spread, rows, even, own_ref, near_ref, far_ref, table_ref, kept_ref):
    flat = own_ref.shape[0] // 3
    high, low, perturb = (
        extend(even, *(ref[index * flat : (index + 1) * flat] for ref in (own_ref, near_ref, far_ref)))
        for index in range(3)
    )
    kept_ref[...] = perturb
    product = own_ref[2 * flat :].astype(F32) * localize(high, low, table_ref, rows)
    total = product[:rows]
    for start in range(rows, flat, rows):
        total = total + product[start : start + rows]
    return spread * total


def partial_kernel(spread, even_ref, own_ref, near_ref, far_ref, table_ref, out_ref, kept_ref):
    even = even_ref[0] == 1
    out_ref[...] = partial_sum(spread, out_ref.shape[0], even, own_ref, near_ref, far_ref, table_ref, kept_ref)


def partial_copies_kernel(spread, rows, even_ref, own_ref, near_ref, far_ref, table_ref, out_ref, kept_ref):
    even = even_ref[0] == 1
    total = partial_sum(spread, rows, even, own_ref, near_ref, far_ref, table_ref, kept_ref)
    for copy in range(out_ref.shape[0]):
        out_ref[copy, :rows] = total
        out_ref[copy, rows:] = jnp.zeros((out_ref.shape[1] - rows, out_ref.shape[2]), F32)


def join_kernel(partial_ref, obs_ref, out_ref):
    rows = partial_ref.shape[0]
    slots = (out_ref.shape[1] - rows) // 2
    total = partial_ref[...]
    turned = jnp.transpose(obs_ref[:, 0, : partial_ref.shape[1]])
    places = jnp.concatenate([turned[:slots], turned[slots : 2 * slots]], axis=1)
    values = jnp.concatenate([turned[2 * slots : 3 * slots], turned[3 * slots : 4 * slots]], axis=1)
    for copy in range(out_ref.shape[0]):
        out_ref[copy, :rows] = total
        out_ref[copy, rows : rows + slots] = places
        out_ref[copy, rows + slots :] = values


def obs_kernel(half, sources, partial_ref, out_ref):
    rows = partial_ref.shape[1] - 2 * half
    field = partial_ref[0, :rows]
    for member in range(1, partial_ref.shape[0]):
        field = field + partial_ref[member, :rows]
    cols = field.shape[1]
    tiles = cols // 2

    def quantity(start, lane):
        parts = [partial_ref[source, rows + start : rows + start + half] for source in sources]
        return jnp.concatenate([part[:, lane : lane + tiles] for part in parts], axis=1)

    at_x, at_y, innov, prec = quantity(0, 0), quantity(0, tiles), quantity(half, 0), quantity(half, tiles)
    corner_col, corner_row = at_x.astype(jnp.int32), at_y.astype(jnp.int32)
    frac_x, frac_y = at_x - corner_col.astype(F32), at_y - corner_row.astype(F32)
    lanes = at_x.shape[1]
    row_at = lax.broadcasted_iota(jnp.int32, (rows, lanes), 0)
    col_at = lax.broadcasted_iota(jnp.int32, (cols, lanes), 0)
    row_parts, col_parts = [], []
    for k in range(half):
        r, x = corner_row[k : k + 1], corner_col[k : k + 1]
        fy, fx = frac_y[k : k + 1], frac_x[k : k + 1]
        row_parts.append(jnp.where(row_at == r, 1.0 - fy, jnp.where(row_at == r + 1, fy, 0.0)))
        col_parts.append(jnp.where(col_at == x, 1.0 - fx, jnp.where(col_at == x + 1, fx, 0.0)))
    row_all = jnp.concatenate(row_parts, axis=1)
    row_high, row_low = split(row_all)
    field_high, field_low = split(jnp.transpose(field))
    picked = jnp.dot(
        jnp.concatenate([field_high, field_low, field_high], axis=1),
        jnp.concatenate([row_high, row_high, row_low], axis=0),
        preferred_element_type=F32,
    )
    weighted = []
    for k in range(half):
        value = jnp.sum(picked[:, k * lanes : (k + 1) * lanes] * col_parts[k], axis=0, keepdims=True)
        weighted.append(prec[k : k + 1] * (value - innov[k : k + 1]))
    weighted = jnp.concatenate(weighted, axis=1)
    rows_high, rows_low = split(row_all * weighted)
    cols_high, cols_low = split(jnp.concatenate(col_parts, axis=1))
    contract = (((1,), (1,)), ((), ()))
    both = jnp.concatenate([rows_high, rows_low], axis=0)
    both = lax.dot_general(both, cols_high, contract, preferred_element_type=F32)
    rest = lax.dot_general(rows_high, cols_low, contract, preferred_element_type=F32)
    out_ref[...] = both[:rows] + both[rows:] + rest


def final_kernel(spread, even_ref, control_ref, own_ref, near_ref, far_ref, kept_ref, table_ref, out_ref):
    even = even_ref[0] == 1
    rows = own_ref.shape[0]
    adjoint = extend(even, own_ref[...], near_ref[...], far_ref[...])
    adjoint = jnp.concatenate([adjoint] * (out_ref.shape[0] // rows), axis=0)
    high, low = split(kept_ref[...].astype(F32) * adjoint)
    out_ref[...] = control_ref[...] + spread * localize(high, low, table_ref, rows)


def call(kernel, out_shapes, scalars, arrays, flops=None):
    specs = [pl.BlockSpec(memory_space=pltpu.SMEM)] * scalars + [pl.BlockSpec(memory_space=pltpu.VMEM)] * arrays
    outs = [jax.ShapeDtypeStruct(shape, dtype) for shape, dtype in out_shapes]
    return pl.pallas_call(
        kernel,
        out_shape=outs,
        in_specs=specs,
        out_specs=[pl.BlockSpec(memory_space=pltpu.VMEM)] * len(outs),
        compiler_params=pltpu.CompilerParams(vmem_limit_bytes=24 * 1024 * 1024),
        cost_estimate=flops and pl.CostEstimate(flops=flops, bytes_accessed=0, transcendentals=0),
    )


def in_hbm(array):
    return pltpu.with_memory_space_constraint(array, pltpu.HBM)


def per_device(perturb, control, obs_cell, obs_count, obs_frac, obs_innov, obs_prec):
    mem_local, levels, row_count, col_count = perturb.shape
    members = lax.axis_size("mem")
    tiles = lax.axis_size("tile")
    spread = 1.0 / math.sqrt(mem_local * members - 1)
    slots = obs_cell.shape[2]
    rows = levels * row_count
    table = jnp.asarray(tables(col_count, row_count, YSCALE, levels))
    even = (1 - lax.axis_index("tile") % 2).astype(jnp.int32).reshape(1)
    member_order = [list(MEMBER_ORDER)]
    near_pairs = [(i, i ^ 1) for i in range(tiles)]
    far_pairs = [(i, (i + 1) % tiles if i % 2 else (i - 1) % tiles) for i in range(tiles)]

    def neighbours(own):
        far = lax.ppermute(own, "tile", far_pairs)
        return lax.ppermute(own, "tile", near_pairs), far

    flat = mem_local * rows
    half = slots // len(ROUTING_PLANES)
    joined = (members, rows + 2 * half, col_count)

    kept = ((flat, 3 * col_count), BF16)
    payload = ((3 * flat, col_count), BF16)

    def route(part, blocks, even, own, weights, table, cell, count, frac, innov, prec):
        size = tiles // len(blocks)
        tile_order = [[block * size + i for block in blocks for i in range(size)]]
        obs = (cell[0].T, count, frac[0].transpose(0, 2, 1), innov[0].T, prec[0].T)
        packed = ((tiles, 1, WIDE * col_count), F32)
        wider = ((3 * flat + FAR_PAD, col_count), BF16)
        pack = call(lambda *refs: pack_kernel(blocks, part, *refs), [payload, wider, packed], 0, 7, 10**9)
        sent, sent_far, packed = pack(*map(in_hbm, (own, weights, *obs)))
        far = lax.ppermute(sent_far, "tile", far_pairs)
        near = lax.ppermute(sent, "tile", near_pairs)
        arrived = lax.all_to_all(
            packed, "tile", split_axis=0, concat_axis=0, tiled=True, axis_index_groups=tile_order
        )
        summing = call(lambda *refs: partial_kernel(spread, *refs), [((rows, col_count), F32), kept], 1, 4, 1000)
        partial, weights = summing(even, sent, near, far, table)
        (partials,) = call(join_kernel, [(joined, F32)], 0, 2)(partial, arrived)
        return partials, weights

    def plain(even, own, weights, table, cell, count, frac, innov, prec):
        (sent,) = call(payload_kernel, [payload], 0, 2, 10**9)(in_hbm(own), in_hbm(weights))
        near, far = neighbours(sent)
        summing = call(lambda *refs: partial_copies_kernel(spread, rows, *refs), [(joined, F32), kept], 1, 4)
        return tuple(summing(even, sent, near, far, table))

    own = control.reshape(flat, col_count)
    weights = perturb.reshape(flat, col_count)
    plane = lax.axis_index("mem")
    branches = [functools.partial(route, part, blocks) for part, blocks in enumerate((FIRST_BLOCKS, SECOND_BLOCKS))]
    which = jnp.where(plane == ROUTING_PLANES[0], 0, jnp.where(plane == ROUTING_PLANES[1], 1, 2))
    partials, weights = lax.switch(
        which, [*branches, plain], even, own, weights, table, obs_cell, obs_count, obs_frac, obs_innov, obs_prec
    )
    partials = lax.all_to_all(
        partials, "mem", split_axis=0, concat_axis=0, tiled=True, axis_index_groups=member_order
    )
    sources = [MEMBER_ORDER.index(plane) for plane in ROUTING_PLANES]
    (adjoint,) = call(lambda *refs: obs_kernel(half, sources, *refs), [((rows, col_count), F32)], 0, 1)(partials)
    near, far = neighbours(adjoint)
    finish = call(lambda *refs: final_kernel(spread, *refs), [((flat, col_count), F32)], 1, 6)
    (gradient,) = finish(even, own, adjoint, near, far, weights, table)
    return gradient.reshape(control.shape)


def solution(mesh):
    return jax.shard_map(
        per_device,
        mesh=mesh,
        in_specs=(
            P("mem", None, None, "tile"),
            P("mem", None, None, "tile"),
            P("tile", None, None),
            P("tile", None),
            P("tile", None, None, None),
            P("tile", None, None),
            P("tile", None, None),
        ),
        out_specs=P("mem", None, None, "tile"),
        check_vma=False,
    )
```

```python
import functools
import math

import jax
import jax.numpy as jnp
import ml_dtypes
import numpy as np
from jax import lax
from jax.experimental import pallas as pl
from jax.experimental.pallas import tpu as pltpu
from jax.sharding import PartitionSpec as P

YSCALE = 1
F32 = jnp.float32
BF16 = jnp.bfloat16
ROUTING_PLANES = (0, 1)
FIRST_BLOCKS = (5, 0, 1, 2, 3, 4, 6, 7)
SECOND_BLOCKS = (5, 0, 7, 2, 4, 6, 1, 3)
WIDE = 3
FAR_PAD = 400
MEMBER_ORDER = (7, 6, 4, 5, 1, 0, 3, 2)


def halves(table):
    high = table.astype(np.float32).astype(ml_dtypes.bfloat16)
    low = (table.astype(np.float32) - high.astype(np.float32)).astype(ml_dtypes.bfloat16)
    return high, low


def tables(col_count, row_count, scale, levels):
    offset = (np.arange(3 * col_count) - col_count)[:, None] - np.arange(col_count)[None, :]
    band = np.where(np.abs(offset) <= col_count, np.exp(-0.5 * (offset / col_count) ** 2), 0.0)
    row_offset = np.arange(row_count)[:, None] - np.arange(row_count)[None, :]
    rows = np.exp(-0.5 * (row_offset / scale) ** 2)
    along_x = np.arange(-col_count, col_count + 1)
    along_y = np.arange(-(row_count - 1), row_count)
    total = np.sum(np.exp(-((along_x / col_count) ** 2))) * np.sum(np.exp(-((along_y / scale) ** 2)))
    mixed = np.kron(np.eye(levels), rows) / np.sqrt(total)
    mixed = np.tile(mixed, (1, col_count // mixed.shape[1]))
    return np.concatenate([*halves(band), *halves(mixed)], axis=0)


def split(values):
    high = values.astype(BF16)
    return high, (values - high.astype(F32)).astype(BF16)


def localize(high, low, table_ref, rows):
    flat, depth = high.shape
    cols = table_ref.shape[1]
    row_block = lax.broadcasted_iota(jnp.int32, (flat, flat), 0) // rows
    same = row_block == lax.broadcasted_iota(jnp.int32, (flat, flat), 1) // rows

    def mixing(start):
        strip = table_ref[start : start + rows].astype(F32)
        strip = jnp.concatenate([strip] * pl.cdiv(flat, cols), axis=1)[:, :flat]
        return jnp.where(same, jnp.concatenate([strip] * (flat // rows), axis=0), 0.0).astype(BF16)

    mixed_high, mixed_low = mixing(2 * depth), mixing(2 * depth + rows)
    band_high, band_low = table_ref[:depth], table_ref[depth : 2 * depth]
    swept = jnp.dot(
        jnp.concatenate([high, low, high], axis=1),
        jnp.concatenate([band_high, band_high, band_low], axis=0),
        preferred_element_type=F32,
    )
    high, low = split(swept)
    both = jnp.dot(mixed_high, jnp.concatenate([high, low], axis=1), preferred_element_type=F32)
    return both[:, :cols] + both[:, cols:] + jnp.dot(mixed_low, high, preferred_element_type=F32)


def extend(even, own, near, far):
    left = jnp.where(even, far, near)
    right = jnp.where(even, near, far)
    return jnp.concatenate([left, own, right], axis=1)


def payload_kernel(own_ref, perturb_ref, out_ref):
    flat = own_ref.shape[0]
    high, low = split(own_ref[...])
    out_ref[:flat] = high
    out_ref[flat : 2 * flat] = low
    out_ref[2 * flat :] = perturb_ref[...]


def pack_kernel(
    blocks, part, own_ref, perturb_ref, cell_ref, count_ref, frac_ref, innov_ref, prec_ref, payload_ref, wider_ref, out_ref
):
    payload_kernel(own_ref, perturb_ref, payload_ref)
    length = payload_ref.shape[0]
    wider_ref[:length] = payload_ref[...]
    wider_ref[length:] = jnp.zeros((wider_ref.shape[0] - length, wider_ref.shape[1]), BF16)
    tiles = innov_ref.shape[1]
    slots = innov_ref.shape[0] // len(ROUTING_PLANES)
    cols = payload_ref.shape[1]
    mine = slice(part * slots, (part + 1) * slots)
    slot = part * slots + lax.broadcasted_iota(jnp.int32, (slots, tiles), 0)
    live = jnp.where(slot < count_ref[...], 1.0, 0.0)
    cell = cell_ref[mine]
    corner_row = lax.shift_right_logical(cell, int(math.log2(cols)))
    corner_col = lax.bitwise_and(cell, cols - 1)
    packed = jnp.concatenate(
        [
            corner_col.astype(F32) + frac_ref[0, mine],
            corner_row.astype(F32) + frac_ref[1, mine],
            innov_ref[mine],
            prec_ref[mine] * live,
            jnp.zeros((cols - 4 * slots, tiles), F32),
        ],
        axis=0,
    )
    turned = jnp.transpose(packed)
    size = tiles // len(blocks)
    for place, block in enumerate(blocks):
        out_ref[place * size : (place + 1) * size, 0, :cols] = turned[block * size : (block + 1) * size]
    out_ref[:, 0, cols:] = jnp.zeros((tiles, out_ref.shape[2] - cols), F32)


def partial_sum(spread, rows, even, own_ref, near_ref, far_ref, table_ref, kept_ref):
    flat = own_ref.shape[0] // 3
    high, low, perturb = (
        extend(even, *(ref[index * flat : (index + 1) * flat] for ref in (own_ref, near_ref, far_ref)))
        for index in range(3)
    )
    kept_ref[...] = perturb
    product = own_ref[2 * flat :].astype(F32) * localize(high, low, table_ref, rows)
    total = product[:rows]
    for start in range(rows, flat, rows):
        total = total + product[start : start + rows]
    return spread * total


def partial_kernel(spread, even_ref, own_ref, near_ref, far_ref, table_ref, out_ref, kept_ref):
    even = even_ref[0] == 1
    out_ref[...] = partial_sum(spread, out_ref.shape[0], even, own_ref, near_ref, far_ref, table_ref, kept_ref)


def partial_copies_kernel(spread, rows, even_ref, own_ref, near_ref, far_ref, table_ref, out_ref, kept_ref):
    even = even_ref[0] == 1
    total = partial_sum(spread, rows, even, own_ref, near_ref, far_ref, table_ref, kept_ref)
    for copy in range(out_ref.shape[0]):
        out_ref[copy, :rows] = total
        out_ref[copy, rows:] = jnp.zeros((out_ref.shape[1] - rows, out_ref.shape[2]), F32)


def join_kernel(partial_ref, obs_ref, out_ref):
    rows = partial_ref.shape[0]
    slots = (out_ref.shape[1] - rows) // 2
    total = partial_ref[...]
    turned = jnp.transpose(obs_ref[:, 0, : partial_ref.shape[1]])
    places = jnp.concatenate([turned[:slots], turned[slots : 2 * slots]], axis=1)
    values = jnp.concatenate([turned[2 * slots : 3 * slots], turned[3 * slots : 4 * slots]], axis=1)
    for copy in range(out_ref.shape[0]):
        out_ref[copy, :rows] = total
        out_ref[copy, rows : rows + slots] = places
        out_ref[copy, rows + slots :] = values


def obs_kernel(half, sources, partial_ref, out_ref):
    rows = partial_ref.shape[1] - 2 * half
    field = partial_ref[0, :rows]
    for member in range(1, partial_ref.shape[0]):
        field = field + partial_ref[member, :rows]
    cols = field.shape[1]
    tiles = cols // 2

    def quantity(start, lane):
        parts = [partial_ref[source, rows + start : rows + start + half] for source in sources]
        return jnp.concatenate([part[:, lane : lane + tiles] for part in parts], axis=1)

    at_x, at_y, innov, prec = quantity(0, 0), quantity(0, tiles), quantity(half, 0), quantity(half, tiles)
    corner_col, corner_row = at_x.astype(jnp.int32), at_y.astype(jnp.int32)
    frac_x, frac_y = at_x - corner_col.astype(F32), at_y - corner_row.astype(F32)
    lanes = at_x.shape[1]
    row_at = lax.broadcasted_iota(jnp.int32, (rows, lanes), 0)
    col_at = lax.broadcasted_iota(jnp.int32, (cols, lanes), 0)
    row_parts, col_parts = [], []
    for k in range(half):
        r, x = corner_row[k : k + 1], corner_col[k : k + 1]
        fy, fx = frac_y[k : k + 1], frac_x[k : k + 1]
        row_parts.append(jnp.where(row_at == r, 1.0 - fy, jnp.where(row_at == r + 1, fy, 0.0)))
        col_parts.append(jnp.where(col_at == x, 1.0 - fx, jnp.where(col_at == x + 1, fx, 0.0)))
    row_all = jnp.concatenate(row_parts, axis=1)
    row_high, row_low = split(row_all)
    field_high, field_low = split(jnp.transpose(field))
    picked = jnp.dot(
        jnp.concatenate([field_high, field_low, field_high], axis=1),
        jnp.concatenate([row_high, row_high, row_low], axis=0),
        preferred_element_type=F32,
    )
    weighted = []
    for k in range(half):
        value = jnp.sum(picked[:, k * lanes : (k + 1) * lanes] * col_parts[k], axis=0, keepdims=True)
        weighted.append(prec[k : k + 1] * (value - innov[k : k + 1]))
    weighted = jnp.concatenate(weighted, axis=1)
    rows_high, rows_low = split(row_all * weighted)
    cols_high, cols_low = split(jnp.concatenate(col_parts, axis=1))
    contract = (((1,), (1,)), ((), ()))
    both = jnp.concatenate([rows_high, rows_low], axis=0)
    both = lax.dot_general(both, cols_high, contract, preferred_element_type=F32)
    rest = lax.dot_general(rows_high, cols_low, contract, preferred_element_type=F32)
    out_ref[...] = both[:rows] + both[rows:] + rest


def final_kernel(spread, even_ref, control_ref, own_ref, near_ref, far_ref, kept_ref, table_ref, out_ref):
    even = even_ref[0] == 1
    rows = own_ref.shape[0]
    adjoint = extend(even, own_ref[...], near_ref[...], far_ref[...])
    adjoint = jnp.concatenate([adjoint] * (out_ref.shape[0] // rows), axis=0)
    high, low = split(kept_ref[...].astype(F32) * adjoint)
    out_ref[...] = control_ref[...] + spread * localize(high, low, table_ref, rows)


def call(kernel, out_shapes, scalars, arrays, flops=None):
    specs = [pl.BlockSpec(memory_space=pltpu.SMEM)] * scalars + [pl.BlockSpec(memory_space=pltpu.VMEM)] * arrays
    outs = [jax.ShapeDtypeStruct(shape, dtype) for shape, dtype in out_shapes]
    return pl.pallas_call(
        kernel,
        out_shape=outs,
        in_specs=specs,
        out_specs=[pl.BlockSpec(memory_space=pltpu.VMEM)] * len(outs),
        compiler_params=pltpu.CompilerParams(vmem_limit_bytes=24 * 1024 * 1024),
        cost_estimate=flops and pl.CostEstimate(flops=flops, bytes_accessed=0, transcendentals=0),
    )


def in_hbm(array):
    return pltpu.with_memory_space_constraint(array, pltpu.HBM)


def per_device(perturb, control, obs_cell, obs_count, obs_frac, obs_innov, obs_prec):
    mem_local, levels, row_count, col_count = perturb.shape
    members = lax.axis_size("mem")
    tiles = lax.axis_size("tile")
    spread = 1.0 / math.sqrt(mem_local * members - 1)
    slots = obs_cell.shape[2]
    rows = levels * row_count
    table = jnp.asarray(tables(col_count, row_count, YSCALE, levels))
    even = (1 - lax.axis_index("tile") % 2).astype(jnp.int32).reshape(1)
    member_order = [list(MEMBER_ORDER)]
    near_pairs = [(i, i ^ 1) for i in range(tiles)]
    far_pairs = [(i, (i + 1) % tiles if i % 2 else (i - 1) % tiles) for i in range(tiles)]

    def neighbours(own):
        far = lax.ppermute(own, "tile", far_pairs)
        return lax.ppermute(own, "tile", near_pairs), far

    flat = mem_local * rows
    half = slots // len(ROUTING_PLANES)
    joined = (members, rows + 2 * half, col_count)

    kept = ((flat, 3 * col_count), BF16)
    payload = ((3 * flat, col_count), BF16)

    def route(part, blocks, even, own, weights, table, cell, count, frac, innov, prec):
        size = tiles // len(blocks)
        tile_order = [[block * size + i for block in blocks for i in range(size)]]
        obs = (cell[0].T, count, frac[0].transpose(0, 2, 1), innov[0].T, prec[0].T)
        packed = ((tiles, 1, WIDE * col_count), F32)
        wider = ((3 * flat + FAR_PAD, col_count), BF16)
        pack = call(lambda *refs: pack_kernel(blocks, part, *refs), [payload, wider, packed], 0, 7, 10**9)
        sent, sent_far, packed = pack(*map(in_hbm, (own, weights, *obs)))
        far = lax.ppermute(sent_far, "tile", far_pairs)
        near = lax.ppermute(sent, "tile", near_pairs)
        arrived = lax.all_to_all(
            packed, "tile", split_axis=0, concat_axis=0, tiled=True, axis_index_groups=tile_order
        )
        summing = call(lambda *refs: partial_kernel(spread, *refs), [((rows, col_count), F32), kept], 1, 4, 1000)
        partial, weights = summing(even, sent, near, far, table)
        (partials,) = call(join_kernel, [(joined, F32)], 0, 2)(partial, arrived)
        return partials, weights

    def plain(even, own, weights, table, cell, count, frac, innov, prec):
        (sent,) = call(payload_kernel, [payload], 0, 2, 10**9)(in_hbm(own), in_hbm(weights))
        near, far = neighbours(sent)
        summing = call(lambda *refs: partial_copies_kernel(spread, rows, *refs), [(joined, F32), kept], 1, 4)
        return tuple(summing(even, sent, near, far, table))

    own = control.reshape(flat, col_count)
    weights = perturb.reshape(flat, col_count)
    plane = lax.axis_index("mem")
    branches = [functools.partial(route, part, blocks) for part, blocks in enumerate((FIRST_BLOCKS, SECOND_BLOCKS))]
    which = jnp.where(plane == ROUTING_PLANES[0], 0, jnp.where(plane == ROUTING_PLANES[1], 1, 2))
    partials, weights = lax.switch(
        which, [*branches, plain], even, own, weights, table, obs_cell, obs_count, obs_frac, obs_innov, obs_prec
    )
    partials = lax.all_to_all(
        partials, "mem", split_axis=0, concat_axis=0, tiled=True, axis_index_groups=member_order
    )
    sources = [MEMBER_ORDER.index(plane) for plane in ROUTING_PLANES]
    (adjoint,) = call(lambda *refs: obs_kernel(half, sources, *refs), [((rows, col_count), F32)], 0, 1)(partials)
    near, far = neighbours(adjoint)
    finish = call(lambda *refs: final_kernel(spread, *refs), [((flat, col_count), F32)], 1, 6)
    (gradient,) = finish(even, own, adjoint, near, far, weights, table)
    return gradient.reshape(control.shape)


def solution(mesh):
    return jax.shard_map(
        per_device,
        mesh=mesh,
        in_specs=(
            P("mem", None, None, "tile"),
            P("mem", None, None, "tile"),
            P("tile", None, None),
            P("tile", None),
            P("tile", None, None, None),
            P("tile", None, None),
            P("tile", None, None),
        ),
        out_specs=P("mem", None, None, "tile"),
        check_vma=False,
    )
```
